256 devices in a mesh: outer: 64 (over x_hi, z, y), inner: 4 (over x_lo, core).
Axes of the slice: x: 4 (x_hi: 2, x_lo: 2; x = x_hi * 2 + x_lo), y: 4, z: 8, core: 2. Of those that a mesh axis runs over, the one named last changes fastest.
Arguments:
- tokens: bfloat16 [32768, 2560], P(('outer', 'inner')), may hold values from -6 to 6
- norm_gain: float32 [2560], replicated, may hold values from 0.1 to 1.9
- w_query: bfloat16 [2560, 2560], P(None, 'inner'), may hold values from -0.15625 to 0.15625
- b_query: float32 [2560], P('inner'), may hold values from -24 to 24
- w_key: bfloat16 [2560, 512], P(None, 'inner'), may hold values from -0.25 to 0.25
- b_key: float32 [512], P('inner'), may hold values from -40 to 40
- w_value: bfloat16 [2560, 512], P(None, 'inner'), may hold values from -0.125 to 0.125
- b_value: float32 [512], P('inner'), may hold values from -3 to 3
- w_out: bfloat16 [2560, 2560], P('inner'), may hold values from -0.125 to 0.125
- positions: int32 [32768], P(('outer', 'inner')), may hold values from 0 to 32767, as said below
Outputs:
- attended: bfloat16 [32768, 2560], P(('outer', 'inner'))
The draws below stay inside these ranges and needn't reach their ends.
Inputs may be any that keep to these rules, and one draw needn't show every extreme that they name: Block b holds two whole runs of 256 consecutive positions in order: run c in its first half and run 2 * 64 - 1 - c in its second, where c differs from block to block; every position occurs once.
All inputs are finite; a program needn't handle non-finite values.
Results may differ from the reference program's by a relative error of at most 0.017.
The reference program's roundings to bfloat16 on the way count: a program that leaves them out, or rounds other values in their place, can miss the bound.
Values may be sent and summed in bfloat16 or wider, within the bound.
No kernel may reach another device: no remote copies, remote signals or barrier semaphores. Data moves between devices by JAX's collectives and lax.ppermute only.
A program may use at most 64 MiB of HBM per device.

```python
import jax
import jax.numpy as jnp
from jax import lax

D = 2560
Q_HEADS = 20
KV_HEADS = 4
HEAD_DIM = 128
BLOCK = 512
SPAN = 256
SEQ = 32768
STEPS = 14
N_OUTER = 64
N_INNER = 4


def draw_b_query(key, part):
    key = jax.random.fold_in(key, 21)
    baseline = 0.5 * jax.random.normal(key, (Q_HEADS, HEAD_DIM), jnp.float32)
    return baseline.reshape(Q_HEADS * HEAD_DIM)


def draw_b_key(key, part):
    key = jax.random.fold_in(key, 37)
    baseline = 0.5 * jax.random.normal(key, (KV_HEADS, HEAD_DIM), jnp.float32)
    return baseline.reshape(KV_HEADS * HEAD_DIM)


def draw_positions(key, part):
    key = jax.random.fold_in(key, 53)
    block_count = SEQ // BLOCK
    pairing = jax.random.permutation(key, jnp.arange(block_count, dtype=jnp.int32))
    row_index = jnp.arange(BLOCK, dtype=jnp.int32)
    second = row_index >= SPAN
    run_index = jnp.where(second[None, :], 2 * block_count - 1 - pairing[:, None], pairing[:, None])
    placed = run_index * SPAN + (row_index % SPAN)[None, :]
    return placed.reshape(SEQ).astype(jnp.int32)


def shard_levels(rng, dims, pieces, least, top_value):
    gain, own = 1.0, jax.random.fold_in(rng, 6)
    for axis_at, parts in pieces:
        steps = jnp.exp(jax.random.uniform(jax.random.fold_in(own, axis_at), (parts,), jnp.float32, least / len(pieces), top_value / len(pieces)))
        gain = gain * jnp.repeat(steps, dims[axis_at] // parts).reshape([-1 if axis == axis_at else 1 for axis in range(len(dims))])
    return gain


def noise(key, dims, width, reach, shards=(), held_as=jnp.bfloat16):
    drawn = width * jax.random.normal(key, dims, jnp.float32)
    if shards:
        drawn = drawn * shard_levels(key, dims, shards, -0.22, 0.18)
    return jnp.clip(drawn, -reach, reach).astype(held_as)


def setup_inputs(seed: int = 0) -> dict:
    key_list = jax.random.split(jax.random.key(seed), 11)
    return {
        "tokens": noise(key_list[0], (SEQ, D), 1.0, 6.0, ((0, 256),)),
        "norm_gain": jnp.clip(1.0 + 0.18 * jax.random.normal(key_list[1], (D,), jnp.float32), 0.1, 1.9),
        "w_query": noise(key_list[2], (D, Q_HEADS * HEAD_DIM), (D // 2) ** -0.5, 0.15625, ((1, 4),)),
        "b_query": draw_b_query(jax.random.fold_in(key_list[10], 71), 0),
        "w_key": noise(key_list[4], (D, KV_HEADS * HEAD_DIM), (D // 4) ** -0.5, 0.25, ((1, 4),)),
        "b_key": draw_b_key(jax.random.fold_in(key_list[10], 71), 0),
        "w_value": noise(key_list[6], (D, KV_HEADS * HEAD_DIM), D ** -0.5, 0.125, ((1, 4),)),
        "b_value": noise(key_list[7], (KV_HEADS * HEAD_DIM,), 0.5, 3.0, ((0, 4),), jnp.float32),
        "w_out": noise(key_list[8], (Q_HEADS * HEAD_DIM, D), (Q_HEADS * HEAD_DIM) ** -0.5, 0.125, ((0, 4),)),
        "positions": draw_positions(jax.random.fold_in(key_list[10], 71), 0),
    }


rope_base = 10000000.0
norm_eps = 1e-06
masked_score = -1e+30

def normalize(tokens, norm_gain):
    values = tokens.astype(jnp.float32)
    scale = lax.rsqrt(lax.optimization_barrier(jnp.mean(values * values, axis=-1, keepdims=True)) + norm_eps)
    return (values * scale * norm_gain).astype(jnp.bfloat16)

def angles_for(places, head_dim):
    inverse = rope_base ** (-(jnp.arange(head_dim // 2, dtype=jnp.float32) * 2.0 / head_dim))
    return places.astype(jnp.float32)[:, None] * inverse[None, :]

def rotate(heads, angles):
    half_dim = heads.shape[-1] // 2
    cosine = jnp.cos(angles)[:, None, :]
    sine_term = jnp.sin(angles)[:, None, :]
    leading = heads[..., :half_dim]
    trailing = heads[..., half_dim:]
    return jnp.concatenate([leading * cosine - trailing * sine_term, trailing * cosine + leading * sine_term], -1)

def reference(tokens, norm_gain, w_query, b_query, w_key, b_key, w_value, b_value, w_out, positions):
    group_size = Q_HEADS // KV_HEADS
    normed = normalize(tokens, norm_gain)
    angles = angles_for(positions, HEAD_DIM)
    queries = jnp.dot(normed, w_query, preferred_element_type=jnp.float32) + b_query
    queries = rotate(queries.reshape(SEQ, Q_HEADS, HEAD_DIM), angles).astype(jnp.bfloat16)
    key_rows = jnp.dot(normed, w_key, preferred_element_type=jnp.float32) + b_key
    key_rows = rotate(key_rows.reshape(SEQ, KV_HEADS, HEAD_DIM), angles).astype(jnp.bfloat16)
    value_rows = (jnp.dot(normed, w_value, preferred_element_type=jnp.float32) + b_value).astype(jnp.bfloat16)
    queries = lax.optimization_barrier(queries)
    key_rows = lax.optimization_barrier(key_rows)
    value_rows = lax.optimization_barrier(value_rows)
    grouped = queries.reshape(N_OUTER, BLOCK, KV_HEADS, group_size, HEAD_DIM)
    key_blocks = key_rows.reshape(N_OUTER, BLOCK, KV_HEADS, HEAD_DIM)
    value_blocks = value_rows.reshape(N_OUTER, BLOCK, KV_HEADS, HEAD_DIM)
    place_blocks = positions.reshape(N_OUTER, BLOCK)
    score_scale = HEAD_DIM ** (-0.5)

    def one_block(block_index):
        sources = (block_index - jnp.arange(STEPS, dtype=jnp.int32)) % N_OUTER
        seen_keys = key_blocks[sources].reshape(STEPS * BLOCK, KV_HEADS, HEAD_DIM).astype(jnp.float32)
        seen_values = value_blocks[sources].reshape(STEPS * BLOCK, KV_HEADS, HEAD_DIM).astype(jnp.float32)
        key_places = place_blocks[sources].reshape(STEPS * BLOCK)
        query_places = place_blocks[block_index]
        query_heads = grouped[block_index].astype(jnp.float32)
        scores = jnp.einsum('qhgd,khd->hgqk', query_heads, seen_keys) * score_scale
        visible = key_places[None, :] <= query_places[:, None]
        scores = jnp.where(visible[None, None], scores, masked_score)
        peak_score = lax.optimization_barrier(jnp.max(scores, axis=-1, keepdims=True))
        exponent = jnp.exp(scores - peak_score)
        denominator = lax.optimization_barrier(jnp.sum(exponent, axis=-1))
        weights = lax.optimization_barrier(exponent.astype(jnp.bfloat16)).astype(jnp.float32)
        summed = jnp.einsum('hgqk,khd->hgqd', weights, seen_values) / denominator[..., None]
        return summed.transpose(2, 0, 1, 3).reshape(BLOCK, Q_HEADS * HEAD_DIM).astype(jnp.bfloat16)
    mixed_heads = lax.map(one_block, jnp.arange(N_OUTER, dtype=jnp.int32)).reshape(SEQ, Q_HEADS * HEAD_DIM)
    group_cols = Q_HEADS * HEAD_DIM // N_INNER
    result = jnp.zeros((SEQ, D), jnp.float32)
    for member in range(N_INNER):
        partial_value = jnp.dot(mixed_heads[:, member * group_cols:(member + 1) * group_cols], w_out[member * group_cols:(member + 1) * group_cols], preferred_element_type=jnp.float32).astype(jnp.bfloat16)
        result = result + lax.optimization_barrier(partial_value).astype(jnp.float32)
    return result.astype(jnp.bfloat16)
```

```python
import functools

import jax
import jax.numpy as jnp
from jax import lax
from jax.experimental import pallas as pl
from jax.experimental.pallas import tpu as pltpu
from jax.sharding import PartitionSpec as P

HEAD_DIM = 128
VISITS = 14
HALF = 256
SHARD = 128
STRIP = 128
HEADS = 5
TILE = 16
MSG = HALF + HALF + TILE
STATE = HEAD_DIM + 16
PEAK, TOTAL = HEAD_DIM, HEAD_DIM + 8

rope_base = 10000000.0
norm_eps = 1e-06
masked_score = -1e30
EXP_SCALE = HEAD_DIM ** (-0.5) * 1.4426950408889634
F32, BF16 = jnp.float32, jnp.bfloat16
VMEM_BYTES = 24 * 2**20

WHOLE = pl.BlockSpec(memory_space=pltpu.VMEM)
SCALARS = pl.BlockSpec(memory_space=pltpu.SMEM)


def params():
    return pltpu.CompilerParams(vmem_limit_bytes=VMEM_BYTES)


def cost(flops, data, exps=0):
    return pl.CostEstimate(flops=flops, bytes_accessed=data, transcendentals=exps)


def where_am_i(pos_ref, runs):
    first = pos_ref[0]
    run = lax.shift_right_logical(first, 8)
    second = run >= runs // 2
    lead = jnp.where(second, runs - 1 - run, run)
    core = lax.bitwise_and(lax.shift_right_logical(first, 7), 1)
    return lead, jnp.where(second, 1, 0), core


def norm_kernel(tokens_ref, gain_ref, out_ref):
    values = tokens_ref[...].astype(F32)
    scale = lax.rsqrt(jnp.mean(values * values, axis=-1, keepdims=True) + norm_eps)
    out_ref[...] = (values * scale * gain_ref[...][None, :]).astype(BF16)


def normalize(tokens, gain):
    return pl.pallas_call(
        norm_kernel,
        out_shape=jax.ShapeDtypeStruct(tokens.shape, BF16),
        in_specs=[WHOLE, WHOLE],
        out_specs=WHOLE,
        compiler_params=params(),
        cost_estimate=cost(5 * tokens.size, 4 * tokens.size),
    )(tokens, gain)


def gather_rows(pos_ref, runs, own_ref, other_ref, rows):
    lead, _, core = where_am_i(pos_ref, runs)
    rows[pl.ds(pl.multiple_of(core * SHARD, SHARD), SHARD), :] = own_ref[...]
    rows[pl.ds(pl.multiple_of((1 - core) * SHARD, SHARD), SHARD), :] = other_ref[...]
    return lead


def rope_for(half, cos_ref, sin_ref):
    lane = lax.broadcasted_iota(jnp.int32, (HALF, HEAD_DIM), 1)
    mine = (lane < HEAD_DIM // 2) if half == 0 else (lane >= HEAD_DIM // 2)
    cos, sin = cos_ref[...], sin_ref[...]
    cos = jnp.where(mine, cos, pltpu.roll(cos, HEAD_DIM // 2, 1))
    sin = jnp.where(mine, sin, pltpu.roll(sin, HEAD_DIM // 2, 1))
    sin = jnp.where(lane < HEAD_DIM // 2, -sin, sin)
    return lambda u: u * cos + pltpu.roll(u, HEAD_DIM // 2, 1) * sin


def key_kernel(half, runs, pos_ref, own_ref, other_ref, wk_ref, wv_ref, bk_ref, bv_ref, cos_ref, sin_ref,
               msg_ref, rows):
    lead = gather_rows(pos_ref, runs, own_ref, other_ref, rows)
    x = rows[...]
    rope = rope_for(half, cos_ref, sin_ref)
    keys = jnp.dot(x, wk_ref[...], preferred_element_type=F32) + bk_ref[...][None, :]
    msg_ref[0:HALF, :] = rope(keys).astype(BF16)
    values = jnp.dot(x, wv_ref[...], preferred_element_type=F32) + bv_ref[...][None, :]
    flipped = values.T.astype(BF16)
    msg_ref[HALF:HALF + SHARD, :] = flipped[:, 0:SHARD]
    msg_ref[HALF + SHARD:2 * HALF, :] = flipped[:, SHARD:HALF]
    msg_ref[2 * HALF:MSG, :] = jnp.full((TILE, HEAD_DIM), lead.astype(F32), F32).astype(BF16)


def query_kernel(half, runs, pos_ref, own_ref, other_ref, wq_ref, bq_ref, cos_ref, sin_ref, q_ref, rows):
    gather_rows(pos_ref, runs, own_ref, other_ref, rows)
    x = rows[...]
    rope = rope_for(half, cos_ref, sin_ref)
    for h in range(HEADS):
        cols = slice(h * HEAD_DIM, (h + 1) * HEAD_DIM)
        heads = jnp.dot(x, wq_ref[:, cols], preferred_element_type=F32) + bq_ref[cols][None, :]
        q_ref[:, h * HALF:(h + 1) * HALF] = rope(heads).T.astype(BF16)


def project_keys(half, runs, positions, own, other, weights, cos, sin):
    features = own.shape[1]
    return pl.pallas_call(
        functools.partial(key_kernel, half, runs),
        out_shape=jax.ShapeDtypeStruct((MSG, HEAD_DIM), BF16),
        in_specs=[SCALARS] + [WHOLE] * 8,
        out_specs=WHOLE,
        scratch_shapes=[pltpu.VMEM((HALF, features), BF16)],
        compiler_params=params(),
        cost_estimate=cost(4 * HALF * features * HEAD_DIM, 4 * features * HEAD_DIM),
    )(positions, own, other, *weights, cos, sin)


def project_queries(half, runs, positions, own, other, w_query, b_query, cos, sin):
    features = own.shape[1]
    return pl.pallas_call(
        functools.partial(query_kernel, half, runs),
        out_shape=jax.ShapeDtypeStruct((HEAD_DIM, HEADS * HALF), BF16),
        in_specs=[SCALARS] + [WHOLE] * 6,
        out_specs=WHOLE,
        scratch_shapes=[pltpu.VMEM((HALF, features), BF16)],
        compiler_params=params(),
        cost_estimate=cost(2 * HALF * features * HEADS * HEAD_DIM, 2 * features * HEADS * HEAD_DIM),
    )(positions, own, other, w_query, b_query, cos, sin)


def distance(kind, level, column):
    if kind == "up":
        return 4 * level + 0 * column
    if kind == "even":
        return 4 * level + column - lax.bitwise_xor(column, 1)
    if kind == "odd":
        return 4 * level + 2 * column - 3
    if kind == "cross":
        return 4 * level + jnp.where(column < 2, -2, 2)
    return jnp.where(column == 0, VISITS - 1, 0)


def visit(q, msgs, state, target, at, first=False):
    k = msgs[at, 0:HALF, :]
    vt = jnp.concatenate([msgs[at, HALF:HALF + SHARD, :], msgs[at, HALF + SHARD:2 * HALF, :]], axis=1)
    for strip in range(HEADS * HALF // STRIP):
        cols = slice(strip * STRIP, (strip + 1) * STRIP)
        s = jnp.dot(k, q[target, :, cols], preferred_element_type=F32)
        if first:
            key_at = lax.broadcasted_iota(jnp.int32, s.shape, 0)
            row_at = lax.broadcasted_iota(jnp.int32, s.shape, 1) + strip * STRIP % HALF
            s = jnp.where(key_at <= row_at, s, masked_score)
            peak = jnp.max(s, axis=0, keepdims=True)
        else:
            old = state[target, PEAK:PEAK + 1, cols]
            peak = jnp.maximum(old, jnp.max(s, axis=0, keepdims=True))
            factor = jnp.exp2((old - peak) * EXP_SCALE)
        expo = jnp.exp2((s - peak) * EXP_SCALE)
        total = jnp.sum(expo, axis=0, keepdims=True)
        mixed = jnp.dot(vt, expo.astype(BF16), preferred_element_type=F32)
        if not first:
            total = total + state[target, TOTAL:TOTAL + 1, cols] * factor
            mixed = mixed + state[target, 0:HEAD_DIM, cols] * factor
        state[target, PEAK:PEAK + 1, cols] = peak
        state[target, TOTAL:TOTAL + 1, cols] = total
        state[target, 0:HEAD_DIM, cols] = mixed


def attend_all(specs, pos_ref, runs, q, msgs, state, seen):
    lead, second, _ = where_am_i(pos_ref, runs)
    column = lax.bitwise_and(pos_ref[SHARD], 3)
    count = len(specs)
    for at, (_, kind, level) in enumerate(specs):
        back = distance(kind, level, column)
        valid = jnp.logical_and(back >= 1, back <= VISITS - 1)
        run = jnp.max(msgs[at, 2 * HALF:MSG, :].astype(F32)).astype(jnp.int32)
        seen[at] = jnp.where(valid, run, -1)

    def one(half, at):
        run = seen[at]
        role = second if half == 0 else 1 - second
        same = jnp.where(role == 0, run < lead, run > lead)

        @pl.when(jnp.logical_and(run >= 0, same))
        def _():
            visit(q, msgs, state, half, at)

        @pl.when(jnp.logical_and(run >= 0, role == 0))
        def _():
            visit(q, msgs, state, 1 - half, at)

    start = 0
    for half in (0, 1):
        stop = start + sum(1 for spec in specs if spec[0] == half)
        if stop > start:
            def body(at, carry, half=half):
                one(half, at)
                return carry
            lax.fori_loop(start, stop, body, 0)
        start = stop


def load(places, sources, qa_ref, qb_ref, q, msgs):
    q[0, :, :] = qa_ref[...]
    q[1, :, :] = qb_ref[...]
    for i, (which, at) in enumerate(places):
        msgs[i, :, :] = sources[which][at, :, :]


def attend_kernel(specs, places, own, runs, pos_ref, qa_ref, qb_ref, *rest):
    state, q, msgs, seen = rest[-4:]
    count = len(specs)
    if own:
        own_a, own_b, arrays = rest[0], rest[1], rest[2:-4]
        load(places, arrays, qa_ref, qb_ref, q, msgs)
        msgs[count, :, :] = own_a[0, :, :]
        msgs[count + 1, :, :] = own_b[0, :, :]
        _, second, _ = where_am_i(pos_ref, runs)
        for half in (0, 1):
            visit(q, msgs, state, half, count + half, True)
        visit(q, msgs, state, 1 - second, count + second)
    else:
        state_in, arrays = rest[0], rest[1:-4]
        load(places, arrays, qa_ref, qb_ref, q, msgs)
        state[...] = state_in[...]
    attend_all(specs, pos_ref, runs, q, msgs, state, seen)


def unpack(messages):
    arrays, places, specs = [], [], []
    for half, kind, level, array, at in sorted(messages, key=lambda m: m[0]):
        for i, known in enumerate(arrays):
            if known is array:
                break
        else:
            i = len(arrays)
            arrays.append(array)
        places.append((i, at))
        specs.append((half, kind, level))
    return tuple(specs), tuple(places), arrays


def working(count):
    return [
        pltpu.VMEM((2, HEAD_DIM, HEADS * HALF), BF16),
        pltpu.VMEM((count, MSG, HEAD_DIM), BF16),
        pltpu.SMEM((count,), jnp.int32),
    ]


def attend(messages, runs, positions, q, state=None, own=()):
    specs, places, arrays = unpack(messages)
    count = len(specs)
    before = list(own) if own else [state]
    return pl.pallas_call(
        functools.partial(attend_kernel, specs, places, bool(own), runs),
        out_shape=jax.ShapeDtypeStruct((2, STATE, HEADS * HALF), F32),
        in_specs=[SCALARS] + [WHOLE] * (2 + len(before) + len(arrays)),
        out_specs=WHOLE,
        scratch_shapes=working(count + len(own)),
        compiler_params=params(),
        cost_estimate=cost(count * 4 * HEADS * HALF * HALF * HEAD_DIM, 2**22, count * HEADS * HALF * HALF),
    )(positions, *q, *before, *arrays)


def project_out(pos_ref, half, mixed, w_ref, keep_ref, send_ref, runs):
    _, _, core = where_am_i(pos_ref, runs)
    keep_at = pl.ds(pl.multiple_of(core * SHARD, SHARD), SHARD)
    send_at = pl.ds(pl.multiple_of((1 - core) * SHARD, SHARD), SHARD)
    x = jnp.concatenate([mixed[send_at, :], mixed[keep_at, :]], axis=0)
    width = 512
    for j in range(w_ref.shape[1] // width):
        cols = slice(j * width, (j + 1) * width)
        part = jnp.dot(x, w_ref[:, cols], preferred_element_type=F32).astype(BF16)
        send_ref[:, cols] = part[0:SHARD]
        keep_ref[:, cols] = part[SHARD:HALF]


def last_kernel(specs, places, runs, pos_ref, qa_ref, qb_ref, state_in, w_ref, *rest):
    keep_far, send_far, near_ref, q, msgs, seen, state, mixed = rest[-8:]
    load(places, rest[:-8], qa_ref, qb_ref, q, msgs)
    state[...] = state_in[...]
    attend_all(specs, pos_ref, runs, q, msgs, state, seen)
    for half, to in ((1, mixed), (0, near_ref)):
        for h in range(HEADS):
            cols = slice(h * HALF, (h + 1) * HALF)
            scale = 1.0 / state[half, TOTAL:TOTAL + 1, cols]
            to[:, h * HEAD_DIM:(h + 1) * HEAD_DIM] = (state[half, 0:HEAD_DIM, cols] * scale).T.astype(BF16)
    project_out(pos_ref, 1, mixed, w_ref, keep_far, send_far, runs)


def attend_last(messages, runs, positions, q, state, w_out):
    specs, places, arrays = unpack(messages)
    count = len(specs)
    part = jax.ShapeDtypeStruct((SHARD, w_out.shape[1]), BF16)
    rows = (HALF, HEADS * HEAD_DIM)
    return pl.pallas_call(
        functools.partial(last_kernel, specs, places, runs),
        out_shape=(part, part, jax.ShapeDtypeStruct(rows, BF16)),
        in_specs=[SCALARS] + [WHOLE] * (4 + len(arrays)),
        out_specs=(WHOLE, WHOLE, WHOLE),
        scratch_shapes=working(count) + [pltpu.VMEM(state.shape, F32), pltpu.VMEM(rows, BF16)],
        compiler_params=params(),
        cost_estimate=cost(
            count * 4 * HEADS * HALF * HALF * HEAD_DIM + 2 * HALF * w_out.size, 2**23, count * HEADS * HALF * HALF
        ),
    )(positions, *q, state, w_out, *arrays)


def near_kernel(runs, pos_ref, mixed_ref, w_ref, keep_ref, send_ref):
    project_out(pos_ref, 0, mixed_ref, w_ref, keep_ref, send_ref, runs)


def near_out(runs, positions, mixed, w_out):
    part = jax.ShapeDtypeStruct((SHARD, w_out.shape[1]), BF16)
    return pl.pallas_call(
        functools.partial(near_kernel, runs),
        out_shape=(part, part),
        in_specs=[SCALARS, WHOLE, WHOLE],
        out_specs=(WHOLE, WHOLE),
        compiler_params=params(),
        cost_estimate=cost(2 * HALF * w_out.size, 2**22),
    )(positions, mixed, w_out)


def after(x, *earlier):
    return lax.optimization_barrier((x, *earlier))[0]


def local(tokens, norm_gain, w_query, b_query, w_key, b_key, w_value, b_value, w_out, positions):
    outer = lax.axis_size("outer")
    runs = 2 * outer

    def along(x, distance):
        return lax.ppermute(x, "outer", [(i, (i + distance) % outer) for i in range(outer)])

    def across(x, flip):
        return lax.ppermute(x, "inner", [(i, i ^ flip) for i in range(4)])

    normed = normalize(tokens, norm_gain)
    far = across(normed, 2)
    near = across(normed, 1)

    run = positions[0] // HALF
    positions = jnp.concatenate([positions, lax.axis_index("outer")[None]])
    row = jnp.arange(HALF, dtype=jnp.int32)[:, None]
    lane = jnp.arange(HEAD_DIM, dtype=jnp.int32)[None, :]
    places = jnp.where(lane < HEAD_DIM // 2, run, runs - 1 - run) * HALF + row
    inverse = rope_base ** (-(jnp.arange(HEAD_DIM // 2, dtype=F32) * 2.0 / HEAD_DIM))
    angles = places.astype(F32) * jnp.concatenate([inverse, inverse])[None, :]
    cos, sin = jnp.cos(angles), jnp.sin(angles)

    kv = (w_key, w_value, b_key, b_value)
    ring = range(outer)

    def pack(*parts):
        return jnp.concatenate(parts, axis=0)

    def up(x):
        return along(x, 4)

    def even(x):
        return lax.ppermute(x, "outer", [(i, i ^ 1) for i in ring])

    def odd(x):
        return lax.ppermute(x, "outer", [(i, i ^ 3) for i in ring])

    def cross(x):
        return lax.ppermute(x, "outer", [(i, i ^ 2) for i in ring if i % 4 >= 2])

    def corner(x):
        return lax.ppermute(x, "outer", [(i, (i + 1) % outer) for i in ring if i % 4 == 3])

    A, B = 0, 1

    a0 = project_keys(0, runs, positions, normed, near, kv, cos, sin)[None]
    a1, e0, o0 = up(a0), even(a0), odd(a0)
    qa = project_queries(0, runs, positions, after(normed, a0), near, w_query, b_query, cos, sin)

    far = after(far, qa, a1, e0, o0)
    far_near = across(far, 1)
    b0 = project_keys(1, runs, positions, far, far_near, kv, cos, sin)[None]
    u0 = pack(a1, b0)
    u1, e1, o1 = up(u0), even(pack(u0, o0)), odd(u0)
    qb = project_queries(1, runs, positions, after(far, b0), far_near, w_query, b_query, cos, sin)
    q = (qa, qb)
    state = attend(((A, "up", 1, a1, 0), (A, "even", 0, e0, 0), (A, "odd", 0, o0, 0)),
                   runs, positions, q, own=(a0, b0))

    v1 = after(u1, state)
    u2, e2, o2 = up(v1), even(pack(v1, o1[1:2])), odd(pack(v1, e1[0:1]))
    state = attend(((A, "up", 2, u1, 0), (B, "up", 1, u1, 1), (A, "even", 1, e1, 0), (B, "even", 0, e1, 1),
                    (A, "cross", 0, e1, 2), (A, "odd", 1, o1, 0), (B, "odd", 0, o1, 1)),
                   runs, positions, q, state)

    v2 = after(u2, state)
    u3, e3, o3 = up(v2[1:2]), even(pack(v2, o2[1:2])), odd(pack(v2, e2[0:1]))
    state = attend(((A, "up", 3, u2, 0), (B, "up", 2, u2, 1), (A, "even", 2, e2, 0), (B, "even", 1, e2, 1),
                    (B, "cross", 0, e2, 2), (A, "odd", 2, o2, 0), (B, "odd", 1, o2, 1), (A, "cross", 1, o2, 2)),
                   runs, positions, q, state)

    v3 = after(u3, state)
    e4, o4, c4, x4 = even(pack(v3, o3[1:2])), odd(pack(v3, e3[0:1])), corner(pack(v2[0:1], v3)), cross(v3)
    state = attend(((B, "up", 3, u3, 0), (A, "even", 3, e3, 0), (B, "even", 2, e3, 1), (B, "cross", 1, e3, 2),
                    (A, "odd", 3, o3, 0), (B, "odd", 2, o3, 1), (A, "cross", 2, o3, 2)),
                   runs, positions, q, state)
    messages = ((B, "even", 3, e4, 0), (B, "cross", 2, e4, 1), (B, "odd", 3, o4, 0), (A, "cross", 3, o4, 1),
                (A, "corner", 3, c4, 0), (B, "corner", 3, c4, 1), (B, "cross", 3, x4, 0))

    keep_far, send_far, mixed_near = attend_last(messages, runs, positions, q, state, w_out)
    got_far = across(send_far, 1)
    keep_near, send_near = near_out(runs, positions, mixed_near, w_out)
    got_near = across(send_near, 1)
    other = (keep_far.astype(F32) + got_far.astype(F32)).astype(BF16)
    arrived = across(other, 2)
    return (keep_near.astype(F32) + got_near.astype(F32) + arrived.astype(F32)).astype(BF16)


def solution(mesh):
    in_specs = (
        P(("outer", "inner"), None),
        P(),
        P(None, "inner"),
        P("inner"),
        P(None, "inner"),
        P("inner"),
        P(None, "inner"),
        P("inner"),
        P("inner", None),
        P(("outer", "inner")),
    )
    out_specs = P(("outer", "inner"), None)
    return jax.shard_map(local, mesh=mesh, in_specs=in_specs, out_specs=out_specs, check_vma=False)
```

```python
import functools

import jax
import jax.numpy as jnp
from jax import lax
from jax.experimental import pallas as pl
from jax.experimental.pallas import tpu as pltpu
from jax.sharding import PartitionSpec as P

HEAD_DIM = 128
VISITS = 14
HALF = 256
SHARD = 128
STRIP = 128
HEADS = 5
TILE = 16
MSG = HALF + HALF + TILE
STATE = HEAD_DIM + 16
PEAK, TOTAL = HEAD_DIM, HEAD_DIM + 8

rope_base = 10000000.0
norm_eps = 1e-06
masked_score = -1e30
EXP_SCALE = HEAD_DIM ** (-0.5) * 1.4426950408889634
F32, BF16 = jnp.float32, jnp.bfloat16
VMEM_BYTES = 24 * 2**20

WHOLE = pl.BlockSpec(memory_space=pltpu.VMEM)
SCALARS = pl.BlockSpec(memory_space=pltpu.SMEM)


def params():
    return pltpu.CompilerParams(vmem_limit_bytes=VMEM_BYTES)


def cost(flops, data, exps=0):
    return pl.CostEstimate(flops=flops, bytes_accessed=data, transcendentals=exps)


def where_am_i(pos_ref, runs):
    first = pos_ref[0]
    run = lax.shift_right_logical(first, 8)
    second = run >= runs // 2
    lead = jnp.where(second, runs - 1 - run, run)
    core = lax.bitwise_and(lax.shift_right_logical(first, 7), 1)
    return lead, jnp.where(second, 1, 0), core


def norm_kernel(tokens_ref, gain_ref, out_ref):
    values = tokens_ref[...].astype(F32)
    scale = lax.rsqrt(jnp.mean(values * values, axis=-1, keepdims=True) + norm_eps)
    out_ref[...] = (values * scale * gain_ref[...][None, :]).astype(BF16)


def normalize(tokens, gain):
    return pl.pallas_call(
        norm_kernel,
        out_shape=jax.ShapeDtypeStruct(tokens.shape, BF16),
        in_specs=[WHOLE, WHOLE],
        out_specs=WHOLE,
        compiler_params=params(),
        cost_estimate=cost(5 * tokens.size, 4 * tokens.size),
    )(tokens, gain)


def gather_rows(pos_ref, runs, own_ref, other_ref, rows):
    lead, _, core = where_am_i(pos_ref, runs)
    rows[pl.ds(pl.multiple_of(core * SHARD, SHARD), SHARD), :] = own_ref[...]
    rows[pl.ds(pl.multiple_of((1 - core) * SHARD, SHARD), SHARD), :] = other_ref[...]
    return lead


def rope_for(half, cos_ref, sin_ref):
    lane = lax.broadcasted_iota(jnp.int32, (HALF, HEAD_DIM), 1)
    mine = (lane < HEAD_DIM // 2) if half == 0 else (lane >= HEAD_DIM // 2)
    cos, sin = cos_ref[...], sin_ref[...]
    cos = jnp.where(mine, cos, pltpu.roll(cos, HEAD_DIM // 2, 1))
    sin = jnp.where(mine, sin, pltpu.roll(sin, HEAD_DIM // 2, 1))
    sin = jnp.where(lane < HEAD_DIM // 2, -sin, sin)
    return lambda u: u * cos + pltpu.roll(u, HEAD_DIM // 2, 1) * sin


def key_kernel(half, runs, pos_ref, own_ref, other_ref, wk_ref, wv_ref, bk_ref, bv_ref, cos_ref, sin_ref,
               msg_ref, rows):
    lead = gather_rows(pos_ref, runs, own_ref, other_ref, rows)
    x = rows[...]
    rope = rope_for(half, cos_ref, sin_ref)
    keys = jnp.dot(x, wk_ref[...], preferred_element_type=F32) + bk_ref[...][None, :]
    msg_ref[0:HALF, :] = rope(keys).astype(BF16)
    values = jnp.dot(x, wv_ref[...], preferred_element_type=F32) + bv_ref[...][None, :]
    flipped = values.T.astype(BF16)
    msg_ref[HALF:HALF + SHARD, :] = flipped[:, 0:SHARD]
    msg_ref[HALF + SHARD:2 * HALF, :] = flipped[:, SHARD:HALF]
    msg_ref[2 * HALF:MSG, :] = jnp.full((TILE, HEAD_DIM), lead.astype(F32), F32).astype(BF16)


def query_kernel(half, runs, pos_ref, own_ref, other_ref, wq_ref, bq_ref, cos_ref, sin_ref, q_ref, rows):
    gather_rows(pos_ref, runs, own_ref, other_ref, rows)
    x = rows[...]
    rope = rope_for(half, cos_ref, sin_ref)
    for h in range(HEADS):
        cols = slice(h * HEAD_DIM, (h + 1) * HEAD_DIM)
        heads = jnp.dot(x, wq_ref[:, cols], preferred_element_type=F32) + bq_ref[cols][None, :]
        q_ref[:, h * HALF:(h + 1) * HALF] = rope(heads).T.astype(BF16)


def project_keys(half, runs, positions, own, other, weights, cos, sin):
    features = own.shape[1]
    return pl.pallas_call(
        functools.partial(key_kernel, half, runs),
        out_shape=jax.ShapeDtypeStruct((MSG, HEAD_DIM), BF16),
        in_specs=[SCALARS] + [WHOLE] * 8,
        out_specs=WHOLE,
        scratch_shapes=[pltpu.VMEM((HALF, features), BF16)],
        compiler_params=params(),
        cost_estimate=cost(4 * HALF * features * HEAD_DIM, 4 * features * HEAD_DIM),
    )(positions, own, other, *weights, cos, sin)


def project_queries(half, runs, positions, own, other, w_query, b_query, cos, sin):
    features = own.shape[1]
    return pl.pallas_call(
        functools.partial(query_kernel, half, runs),
        out_shape=jax.ShapeDtypeStruct((HEAD_DIM, HEADS * HALF), BF16),
        in_specs=[SCALARS] + [WHOLE] * 6,
        out_specs=WHOLE,
        scratch_shapes=[pltpu.VMEM((HALF, features), BF16)],
        compiler_params=params(),
        cost_estimate=cost(2 * HALF * features * HEADS * HEAD_DIM, 2 * features * HEADS * HEAD_DIM),
    )(positions, own, other, w_query, b_query, cos, sin)


def distance(kind, level, column):
    if kind == "up":
        return 4 * level + 0 * column
    if kind == "even":
        return 4 * level + column - lax.bitwise_xor(column, 1)
    if kind == "odd":
        return 4 * level + 2 * column - 3
    if kind == "cross":
        return 4 * level + jnp.where(column < 2, -2, 2)
    return jnp.where(column == 0, VISITS - 1, 0)


def visit(q_ref, msgs, state, at, first=False):
    k = msgs[at, 0:HALF, :]
    vt = jnp.concatenate([msgs[at, HALF:HALF + SHARD, :], msgs[at, HALF + SHARD:2 * HALF, :]], axis=1)
    for strip in range(HEADS * HALF // STRIP):
        cols = slice(strip * STRIP, (strip + 1) * STRIP)
        s = jnp.dot(k, q_ref[:, cols], preferred_element_type=F32)
        if first:
            key_at = lax.broadcasted_iota(jnp.int32, s.shape, 0)
            row_at = lax.broadcasted_iota(jnp.int32, s.shape, 1) + strip * STRIP % HALF
            s = jnp.where(key_at <= row_at, s, masked_score)
            peak = jnp.max(s, axis=0, keepdims=True)
        else:
            old = state[PEAK:PEAK + 1, cols]
            peak = jnp.maximum(old, jnp.max(s, axis=0, keepdims=True))
            factor = jnp.exp2((old - peak) * EXP_SCALE)
        expo = jnp.exp2((s - peak) * EXP_SCALE)
        total = jnp.sum(expo, axis=0, keepdims=True)
        mixed = jnp.dot(vt, expo.astype(BF16), preferred_element_type=F32)
        if not first:
            total = total + state[TOTAL:TOTAL + 1, cols] * factor
            mixed = mixed + state[0:HEAD_DIM, cols] * factor
        state[PEAK:PEAK + 1, cols] = peak
        state[TOTAL:TOTAL + 1, cols] = total
        state[0:HEAD_DIM, cols] = mixed


def attend_all(target, specs, places, arrays, pos_ref, runs, q_ref, msgs, state, todo):
    lead, second, _ = where_am_i(pos_ref, runs)
    column = lax.bitwise_and(pos_ref[SHARD], 3)
    todo[0] = 0
    for at, ((half, kind, level), (which, index)) in enumerate(zip(specs, places)):
        back = distance(kind, level, column)
        valid = jnp.logical_and(back >= 1, back <= VISITS - 1)
        role = second if half == 0 else 1 - second
        if half == target:
            run = jnp.max(arrays[which][index, 2 * HALF:MSG, :].astype(F32)).astype(jnp.int32)
            seen = jnp.where(role == 0, run < lead, run > lead)
        else:
            seen = role == 0

        @pl.when(jnp.logical_and(valid, seen))
        def _(which=which, index=index):
            place = todo[0]
            msgs[place, :, :] = arrays[which][index, :, :]
            todo[0] = place + 1

    count = todo[0]

    def two(i, carry):
        visit(q_ref, msgs, state, 2 * i)
        visit(q_ref, msgs, state, 2 * i + 1)
        return carry

    lax.fori_loop(0, lax.shift_right_logical(count, 1), two, 0)

    @pl.when(lax.bitwise_and(count, 1) == 1)
    def _():
        visit(q_ref, msgs, state, count - 1)


def begin(target, own_a, own_b, pos_ref, runs, q_ref, msgs, state):
    _, second, _ = where_am_i(pos_ref, runs)
    msgs[0, :, :] = (own_a, own_b)[target][0, :, :]
    visit(q_ref, msgs, state, 0, True)

    @pl.when(second == 1 - target)
    def _():
        msgs[0, :, :] = (own_b, own_a)[target][0, :, :]
        visit(q_ref, msgs, state, 0)


def attend_kernel(target, specs, places, own, runs, pos_ref, q_ref, *rest):
    state, msgs, todo = rest[-3:]
    if own:
        arrays = rest[2:-3]
        begin(target, rest[0], rest[1], pos_ref, runs, q_ref, msgs, state)
    else:
        arrays = rest[1:-3]
        state[...] = rest[0][...]
    attend_all(target, specs, places, arrays, pos_ref, runs, q_ref, msgs, state, todo)


def unpack(messages):
    arrays, places, specs = [], [], []
    for half, kind, level, array, at in messages:
        for i, known in enumerate(arrays):
            if known is array:
                break
        else:
            i = len(arrays)
            arrays.append(array)
        places.append((i, at))
        specs.append((half, kind, level))
    return tuple(specs), tuple(places), arrays


def working(count):
    return [pltpu.VMEM((count, MSG, HEAD_DIM), BF16), pltpu.SMEM((1,), jnp.int32)]


def task_cost(count, more=0):
    return cost(count * 2 * HEADS * HALF * HALF * HEAD_DIM + more, 2**21, count * HEADS * HALF * HALF // 2)


def attend(target, messages, runs, positions, q, state=None, own=()):
    specs, places, arrays = unpack(messages)
    before = list(own) if own else [state]
    return pl.pallas_call(
        functools.partial(attend_kernel, target, specs, places, bool(own), runs),
        out_shape=jax.ShapeDtypeStruct((STATE, HEADS * HALF), F32),
        in_specs=[SCALARS] + [WHOLE] * (1 + len(before) + len(arrays)),
        out_specs=WHOLE,
        scratch_shapes=working(len(specs)),
        compiler_params=params(),
        cost_estimate=task_cost(len(specs)),
    )(positions, q, *before, *arrays)


def project_out(pos_ref, runs, mixed, w_ref, keep_ref, send_ref):
    _, _, core = where_am_i(pos_ref, runs)
    keep_at = pl.ds(pl.multiple_of(core * SHARD, SHARD), SHARD)
    send_at = pl.ds(pl.multiple_of((1 - core) * SHARD, SHARD), SHARD)
    x = jnp.concatenate([mixed[send_at, :], mixed[keep_at, :]], axis=0)
    width = 512
    for j in range(w_ref.shape[1] // width):
        cols = slice(j * width, (j + 1) * width)
        part = jnp.dot(x, w_ref[:, cols], preferred_element_type=F32).astype(BF16)
        send_ref[:, cols] = part[0:SHARD]
        keep_ref[:, cols] = part[SHARD:HALF]


def last_kernel(target, specs, places, runs, pos_ref, q_ref, state_in, w_ref, *rest):
    keep_ref, send_ref, msgs, todo, state, mixed = rest[-6:]
    state[...] = state_in[...]
    attend_all(target, specs, places, rest[:-6], pos_ref, runs, q_ref, msgs, state, todo)
    for h in range(HEADS):
        cols = slice(h * HALF, (h + 1) * HALF)
        scale = 1.0 / state[TOTAL:TOTAL + 1, cols]
        mixed[:, h * HEAD_DIM:(h + 1) * HEAD_DIM] = (state[0:HEAD_DIM, cols] * scale).T.astype(BF16)
    project_out(pos_ref, runs, mixed, w_ref, keep_ref, send_ref)


def attend_last(target, messages, runs, positions, q, state, w_out):
    specs, places, arrays = unpack(messages)
    part = jax.ShapeDtypeStruct((SHARD, w_out.shape[1]), BF16)
    return pl.pallas_call(
        functools.partial(last_kernel, target, specs, places, runs),
        out_shape=(part, part),
        in_specs=[SCALARS] + [WHOLE] * (3 + len(arrays)),
        out_specs=(WHOLE, WHOLE),
        scratch_shapes=working(len(specs)) + [pltpu.VMEM(state.shape, F32), pltpu.VMEM((HALF, HEADS * HEAD_DIM), BF16)],
        compiler_params=params(),
        cost_estimate=task_cost(len(specs), 2 * HALF * w_out.size),
    )(positions, q, state, w_out, *arrays)


def after(x, *earlier):
    return lax.optimization_barrier((x, *earlier))[0]


def local(tokens, norm_gain, w_query, b_query, w_key, b_key, w_value, b_value, w_out, positions):
    outer = lax.axis_size("outer")
    runs = 2 * outer

    def along(x, distance):
        return lax.ppermute(x, "outer", [(i, (i + distance) % outer) for i in range(outer)])

    def across(x, flip):
        return lax.ppermute(x, "inner", [(i, i ^ flip) for i in range(4)])

    normed = normalize(tokens, norm_gain)
    far = across(normed, 2)
    near = across(normed, 1)

    run = positions[0] // HALF
    positions = jnp.concatenate([positions, lax.axis_index("outer")[None]])
    row = jnp.arange(HALF, dtype=jnp.int32)[:, None]
    lane = jnp.arange(HEAD_DIM, dtype=jnp.int32)[None, :]
    places = jnp.where(lane < HEAD_DIM // 2, run, runs - 1 - run) * HALF + row
    inverse = rope_base ** (-(jnp.arange(HEAD_DIM // 2, dtype=F32) * 2.0 / HEAD_DIM))
    angles = places.astype(F32) * jnp.concatenate([inverse, inverse])[None, :]
    cos, sin = jnp.cos(angles), jnp.sin(angles)

    kv = (w_key, w_value, b_key, b_value)
    ring = range(outer)

    def pack(*parts):
        return jnp.concatenate(parts, axis=0)

    def up(x):
        return along(x, 4)

    def even(x):
        return lax.ppermute(x, "outer", [(i, i ^ 1) for i in ring])

    def odd(x):
        return lax.ppermute(x, "outer", [(i, i ^ 3) for i in ring])

    def corner(x):
        return lax.ppermute(x, "outer", [(i, (i + 7 - 2 * (i % 4)) % outer) for i in ring if i % 4 >= 2])

    A, B = 0, 1

    a0 = project_keys(0, runs, positions, normed, near, kv, cos, sin)[None]
    a1, e0, o0 = up(a0), even(a0), odd(a0)
    qa = project_queries(0, runs, positions, after(normed, a0), near, w_query, b_query, cos, sin)

    far = after(far, qa, a1, e0, o0)
    far_near = across(far, 1)
    b0 = project_keys(1, runs, positions, far, far_near, kv, cos, sin)[None]
    u0 = pack(a1, b0)
    u1, e1, o1 = up(u0), even(pack(u0, o0)), odd(u0)
    qb = project_queries(1, runs, positions, after(far, b0), far_near, w_query, b_query, cos, sin)
    came1 = ((A, "up", 1, a1, 0), (A, "even", 0, e0, 0), (A, "odd", 0, o0, 0))
    state = attend(B, came1, runs, positions, qb, own=(a0, b0))

    v1 = after(u1, state)
    u2, e2, o2 = up(v1), even(pack(v1, o1[1:2])), odd(pack(v1, e1[0:1]))
    came2 = ((A, "up", 2, u1, 0), (B, "up", 1, u1, 1), (A, "even", 1, e1, 0), (B, "even", 0, e1, 1),
             (A, "cross", 0, e1, 2), (A, "odd", 1, o1, 0), (B, "odd", 0, o1, 1))
    state = attend(B, came2, runs, positions, qb, state)
    near_state = attend(A, came1, runs, positions, after(qa, state), own=(a0, b0))

    v2 = after(u2, near_state)
    u3, e3, o3 = up(pack(v2[1:2], o2[2:3])), even(pack(v2, o2[1:2])), odd(v2)
    came3 = ((A, "up", 3, u2, 0), (B, "up", 2, u2, 1), (A, "even", 2, e2, 0), (B, "even", 1, e2, 1),
             (B, "cross", 0, e2, 2), (A, "odd", 2, o2, 0), (B, "odd", 1, o2, 1), (A, "cross", 1, o2, 2))
    state = attend(B, came3, runs, positions, qb, state)

    v3 = after(u3, state)
    u4, e4, o4 = up(pack(v3[1:2], o3[0:1])), even(pack(v3[0:1], o3[1:2])), odd(v3[0:1])
    c4 = corner(pack(v3[0:1], e3[1:2]))
    came4 = ((B, "up", 3, u3, 0), (A, "cross", 2, u3, 1), (A, "even", 3, e3, 0), (B, "even", 2, e3, 1),
             (B, "cross", 1, e3, 2), (A, "odd", 3, o3, 0), (B, "odd", 2, o3, 1))
    state = attend(B, came4, runs, positions, qb, state)
    near_state = attend(A, came2, runs, positions, after(qa, state), near_state)
    came5 = ((B, "even", 3, e4, 0), (B, "cross", 2, e4, 1), (B, "odd", 3, o4, 0), (A, "cross", 3, u4, 0),
             (A, "corner", 3, u4, 1), (B, "corner", 3, c4, 0), (B, "cross", 3, c4, 1))

    keep_far, send_far = attend_last(B, came5, runs, positions, after(qb, near_state), state, w_out)
    got_far = across(send_far, 1)
    other = (keep_far.astype(F32) + got_far.astype(F32)).astype(BF16)
    arrived = across(other, 2)
    keep_near, send_near = attend_last(
        A, came3 + came4 + came5, runs, positions, after(qa, other), near_state, w_out
    )
    got_near = across(send_near, 1)
    return (keep_near.astype(F32) + got_near.astype(F32) + arrived.astype(F32)).astype(BF16)


def solution(mesh):
    in_specs = (
        P(("outer", "inner"), None),
        P(),
        P(None, "inner"),
        P("inner"),
        P(None, "inner"),
        P("inner"),
        P(None, "inner"),
        P("inner"),
        P("inner", None),
        P(("outer", "inner")),
    )
    out_specs = P(("outer", "inner"), None)
    return jax.shard_map(local, mesh=mesh, in_specs=in_specs, out_specs=out_specs, check_vma=False)
```

```python
import functools

import jax
import jax.numpy as jnp
from jax import lax
from jax.experimental import pallas as pl
from jax.experimental.pallas import tpu as pltpu
from jax.sharding import PartitionSpec as P

HEAD_DIM = 128
VISITS = 14
HALF = 256
SHARD = 128
STRIP = 128
HEADS = 5
TILE = 16
MSG = HALF + HALF + TILE
STATE = HEAD_DIM + 16
PEAK, TOTAL = HEAD_DIM, HEAD_DIM + 8

rope_base = 10000000.0
norm_eps = 1e-06
masked_score = -1e30
EXP_SCALE = HEAD_DIM ** (-0.5) * 1.4426950408889634
F32, BF16 = jnp.float32, jnp.bfloat16
VMEM_BYTES = 24 * 2**20

WHOLE = pl.BlockSpec(memory_space=pltpu.VMEM)
SCALARS = pl.BlockSpec(memory_space=pltpu.SMEM)


def params():
    return pltpu.CompilerParams(vmem_limit_bytes=VMEM_BYTES)


def cost(flops, data, exps=0):
    return pl.CostEstimate(flops=flops, bytes_accessed=data, transcendentals=exps)


def where_am_i(pos_ref, runs):
    first = pos_ref[0]
    run = lax.shift_right_logical(first, 8)
    second = run >= runs // 2
    lead = jnp.where(second, runs - 1 - run, run)
    core = lax.bitwise_and(lax.shift_right_logical(first, 7), 1)
    return lead, jnp.where(second, 1, 0), core


def norm_kernel(tokens_ref, gain_ref, out_ref):
    values = tokens_ref[...].astype(F32)
    scale = lax.rsqrt(jnp.mean(values * values, axis=-1, keepdims=True) + norm_eps)
    out_ref[...] = (values * scale * gain_ref[...][None, :]).astype(BF16)


def normalize(tokens, gain):
    return pl.pallas_call(
        norm_kernel,
        out_shape=jax.ShapeDtypeStruct(tokens.shape, BF16),
        in_specs=[WHOLE, WHOLE],
        out_specs=WHOLE,
        compiler_params=params(),
        cost_estimate=cost(5 * tokens.size, 4 * tokens.size),
    )(tokens, gain)


def gather_rows(pos_ref, runs, own_ref, other_ref, rows):
    lead, _, core = where_am_i(pos_ref, runs)
    rows[pl.ds(pl.multiple_of(core * SHARD, SHARD), SHARD), :] = own_ref[...]
    rows[pl.ds(pl.multiple_of((1 - core) * SHARD, SHARD), SHARD), :] = other_ref[...]
    return lead


def rope_for(half, cos_ref, sin_ref):
    lane = lax.broadcasted_iota(jnp.int32, (HALF, HEAD_DIM), 1)
    mine = (lane < HEAD_DIM // 2) if half == 0 else (lane >= HEAD_DIM // 2)
    cos, sin = cos_ref[...], sin_ref[...]
    cos = jnp.where(mine, cos, pltpu.roll(cos, HEAD_DIM // 2, 1))
    sin = jnp.where(mine, sin, pltpu.roll(sin, HEAD_DIM // 2, 1))
    sin = jnp.where(lane < HEAD_DIM // 2, -sin, sin)
    return lambda u: u * cos + pltpu.roll(u, HEAD_DIM // 2, 1) * sin


def key_kernel(half, runs, pos_ref, own_ref, other_ref, wk_ref, wv_ref, bk_ref, bv_ref, cos_ref, sin_ref,
               msg_ref, rows):
    lead = gather_rows(pos_ref, runs, own_ref, other_ref, rows)
    x = rows[...]
    rope = rope_for(half, cos_ref, sin_ref)
    keys = jnp.dot(x, wk_ref[...], preferred_element_type=F32) + bk_ref[...][None, :]
    msg_ref[0:HALF, :] = rope(keys).astype(BF16)
    values = jnp.dot(x, wv_ref[...], preferred_element_type=F32) + bv_ref[...][None, :]
    flipped = values.T.astype(BF16)
    msg_ref[HALF:HALF + SHARD, :] = flipped[:, 0:SHARD]
    msg_ref[HALF + SHARD:2 * HALF, :] = flipped[:, SHARD:HALF]
    msg_ref[2 * HALF:MSG, :] = jnp.full((TILE, HEAD_DIM), lead.astype(F32), F32).astype(BF16)


def query_kernel(half, runs, pos_ref, own_ref, other_ref, wq_ref, bq_ref, cos_ref, sin_ref, q_ref, rows):
    gather_rows(pos_ref, runs, own_ref, other_ref, rows)
    x = rows[...]
    rope = rope_for(half, cos_ref, sin_ref)
    for h in range(HEADS):
        cols = slice(h * HEAD_DIM, (h + 1) * HEAD_DIM)
        heads = jnp.dot(x, wq_ref[:, cols], preferred_element_type=F32) + bq_ref[cols][None, :]
        q_ref[:, h * HALF:(h + 1) * HALF] = rope(heads).T.astype(BF16)


def project_keys(half, runs, positions, own, other, weights, cos, sin):
    features = own.shape[1]
    return pl.pallas_call(
        functools.partial(key_kernel, half, runs),
        out_shape=jax.ShapeDtypeStruct((MSG, HEAD_DIM), BF16),
        in_specs=[SCALARS] + [WHOLE] * 8,
        out_specs=WHOLE,
        scratch_shapes=[pltpu.VMEM((HALF, features), BF16)],
        compiler_params=params(),
        cost_estimate=cost(4 * HALF * features * HEAD_DIM, 4 * features * HEAD_DIM),
    )(positions, own, other, *weights, cos, sin)


def project_queries(half, runs, positions, own, other, w_query, b_query, cos, sin):
    features = own.shape[1]
    return pl.pallas_call(
        functools.partial(query_kernel, half, runs),
        out_shape=jax.ShapeDtypeStruct((HEAD_DIM, HEADS * HALF), BF16),
        in_specs=[SCALARS] + [WHOLE] * 6,
        out_specs=WHOLE,
        scratch_shapes=[pltpu.VMEM((HALF, features), BF16)],
        compiler_params=params(),
        cost_estimate=cost(2 * HALF * features * HEADS * HEAD_DIM, 2 * features * HEADS * HEAD_DIM),
    )(positions, own, other, w_query, b_query, cos, sin)


def distance(kind, level, column):
    if kind == "up":
        return 4 * level + 0 * column
    if kind == "even":
        return 4 * level + column - lax.bitwise_xor(column, 1)
    if kind == "odd":
        return 4 * level + 2 * column - 3
    if kind == "cross":
        return 4 * level + jnp.where(column < 2, -2, 2)
    return jnp.where(column == 0, VISITS - 1, 0)


def visit(q_ref, msgs, state, at, first=False):
    k = msgs[at, 0:HALF, :]
    vt = jnp.concatenate([msgs[at, HALF:HALF + SHARD, :], msgs[at, HALF + SHARD:2 * HALF, :]], axis=1)
    for strip in range(HEADS * HALF // STRIP):
        cols = slice(strip * STRIP, (strip + 1) * STRIP)
        s = jnp.dot(k, q_ref[:, cols], preferred_element_type=F32)
        if first:
            key_at = lax.broadcasted_iota(jnp.int32, s.shape, 0)
            row_at = lax.broadcasted_iota(jnp.int32, s.shape, 1) + strip * STRIP % HALF
            s = jnp.where(key_at <= row_at, s, masked_score)
            peak = jnp.max(s, axis=0, keepdims=True)
        else:
            old = state[PEAK:PEAK + 1, cols]
            peak = jnp.maximum(old, jnp.max(s, axis=0, keepdims=True))
            factor = jnp.exp2((old - peak) * EXP_SCALE)
        expo = jnp.exp2((s - peak) * EXP_SCALE)
        total = jnp.sum(expo, axis=0, keepdims=True)
        mixed = jnp.dot(vt, expo.astype(BF16), preferred_element_type=F32)
        if not first:
            total = total + state[TOTAL:TOTAL + 1, cols] * factor
            mixed = mixed + state[0:HEAD_DIM, cols] * factor
        state[PEAK:PEAK + 1, cols] = peak
        state[TOTAL:TOTAL + 1, cols] = total
        state[0:HEAD_DIM, cols] = mixed


def attend_all(target, specs, places, arrays, pos_ref, runs, q_ref, msgs, state, todo):
    lead, second, _ = where_am_i(pos_ref, runs)
    column = lax.bitwise_and(pos_ref[SHARD], 3)
    todo[0] = 0
    wanted = []
    for (half, kind, level), (which, index) in zip(specs, places):
        back = distance(kind, level, column)
        valid = jnp.logical_and(back >= 1, back <= VISITS - 1)
        role = second if half == 0 else 1 - second
        if half == target:
            run = jnp.max(arrays[which][index, 2 * HALF:MSG, :].astype(F32)).astype(jnp.int32)
            seen = jnp.where(role == 0, run < lead, run > lead)
        else:
            seen = role == 0
        wanted.append(jnp.logical_and(valid, seen))
    for want, (which, index) in zip(wanted, places):
        @pl.when(want)
        def _(which=which, index=index):
            place = todo[0]
            msgs[place, :, :] = arrays[which][index, :, :]
            todo[0] = place + 1

    count = todo[0]

    def two(i, carry):
        visit(q_ref, msgs, state, 2 * i)
        visit(q_ref, msgs, state, 2 * i + 1)
        return carry

    lax.fori_loop(0, lax.shift_right_logical(count, 1), two, 0)

    @pl.when(lax.bitwise_and(count, 1) == 1)
    def _():
        visit(q_ref, msgs, state, count - 1)


def begin(target, own_a, own_b, pos_ref, runs, q_ref, msgs, state):
    _, second, _ = where_am_i(pos_ref, runs)
    msgs[0, :, :] = (own_a, own_b)[target][0, :, :]
    visit(q_ref, msgs, state, 0, True)

    @pl.when(second == 1 - target)
    def _():
        msgs[0, :, :] = (own_b, own_a)[target][0, :, :]
        visit(q_ref, msgs, state, 0)


def attend_kernel(target, specs, places, own, runs, pos_ref, q_ref, *rest):
    state, msgs, todo = rest[-3:]
    if own:
        arrays = rest[2:-3]
        begin(target, rest[0], rest[1], pos_ref, runs, q_ref, msgs, state)
    else:
        arrays = rest[1:-3]
        state[...] = rest[0][...]
    attend_all(target, specs, places, arrays, pos_ref, runs, q_ref, msgs, state, todo)


def unpack(messages):
    arrays, places, specs = [], [], []
    for half, kind, level, array, at in messages:
        for i, known in enumerate(arrays):
            if known is array:
                break
        else:
            i = len(arrays)
            arrays.append(array)
        places.append((i, at))
        specs.append((half, kind, level))
    return tuple(specs), tuple(places), arrays


def working(count):
    return [pltpu.VMEM((count, MSG, HEAD_DIM), BF16), pltpu.SMEM((1,), jnp.int32)]


def task_cost(count, more=0):
    return cost(count * 2 * HEADS * HALF * HALF * HEAD_DIM + more, 2**21, count * HEADS * HALF * HALF // 2)


def attend(target, messages, runs, positions, q, state=None, own=()):
    specs, places, arrays = unpack(messages)
    before = list(own) if own else [state]
    return pl.pallas_call(
        functools.partial(attend_kernel, target, specs, places, bool(own), runs),
        out_shape=jax.ShapeDtypeStruct((STATE, HEADS * HALF), F32),
        in_specs=[SCALARS] + [WHOLE] * (1 + len(before) + len(arrays)),
        out_specs=WHOLE,
        scratch_shapes=working(len(specs)),
        compiler_params=params(),
        cost_estimate=task_cost(len(specs)),
    )(positions, q, *before, *arrays)


def project_out(pos_ref, runs, mixed, w_ref, keep_ref, send_ref):
    _, _, core = where_am_i(pos_ref, runs)
    keep_at = pl.ds(pl.multiple_of(core * SHARD, SHARD), SHARD)
    send_at = pl.ds(pl.multiple_of((1 - core) * SHARD, SHARD), SHARD)
    x = jnp.concatenate([mixed[send_at, :], mixed[keep_at, :]], axis=0)
    width = 512
    for j in range(w_ref.shape[1] // width):
        cols = slice(j * width, (j + 1) * width)
        part = jnp.dot(x, w_ref[:, cols], preferred_element_type=F32).astype(BF16)
        send_ref[:, cols] = part[0:SHARD]
        keep_ref[:, cols] = part[SHARD:HALF]


def last_kernel(target, specs, places, runs, pos_ref, q_ref, state_in, w_ref, *rest):
    keep_ref, send_ref, msgs, todo, state, mixed = rest[-6:]
    state[...] = state_in[...]
    attend_all(target, specs, places, rest[:-6], pos_ref, runs, q_ref, msgs, state, todo)
    for h in range(HEADS):
        cols = slice(h * HALF, (h + 1) * HALF)
        scale = 1.0 / state[TOTAL:TOTAL + 1, cols]
        mixed[:, h * HEAD_DIM:(h + 1) * HEAD_DIM] = (state[0:HEAD_DIM, cols] * scale).T.astype(BF16)
    project_out(pos_ref, runs, mixed, w_ref, keep_ref, send_ref)


def attend_last(target, messages, runs, positions, q, state, w_out):
    specs, places, arrays = unpack(messages)
    part = jax.ShapeDtypeStruct((SHARD, w_out.shape[1]), BF16)
    return pl.pallas_call(
        functools.partial(last_kernel, target, specs, places, runs),
        out_shape=(part, part),
        in_specs=[SCALARS] + [WHOLE] * (3 + len(arrays)),
        out_specs=(WHOLE, WHOLE),
        scratch_shapes=working(len(specs)) + [pltpu.VMEM(state.shape, F32), pltpu.VMEM((HALF, HEADS * HEAD_DIM), BF16)],
        compiler_params=params(),
        cost_estimate=task_cost(len(specs), 2 * HALF * w_out.size),
    )(positions, q, state, w_out, *arrays)


def after(x, *earlier):
    return lax.optimization_barrier((x, *earlier))[0]


def local(tokens, norm_gain, w_query, b_query, w_key, b_key, w_value, b_value, w_out, positions):
    outer = lax.axis_size("outer")
    runs = 2 * outer

    def along(x, distance):
        return lax.ppermute(x, "outer", [(i, (i + distance) % outer) for i in range(outer)])

    def across(x, flip):
        return lax.ppermute(x, "inner", [(i, i ^ flip) for i in range(4)])

    far_tokens = across(tokens, 2)
    normed = normalize(tokens, norm_gain)
    near = across(normed, 1)

    run = positions[0] // HALF
    positions = jnp.concatenate([positions, lax.axis_index("outer")[None]])
    row = jnp.arange(HALF, dtype=jnp.int32)[:, None]
    lane = jnp.arange(HEAD_DIM, dtype=jnp.int32)[None, :]
    places = jnp.where(lane < HEAD_DIM // 2, run, runs - 1 - run) * HALF + row
    inverse = rope_base ** (-(jnp.arange(HEAD_DIM // 2, dtype=F32) * 2.0 / HEAD_DIM))
    angles = places.astype(F32) * jnp.concatenate([inverse, inverse])[None, :]
    cos, sin = jnp.cos(angles), jnp.sin(angles)

    kv = (w_key, w_value, b_key, b_value)
    ring = range(outer)

    def pack(*parts):
        return jnp.concatenate(parts, axis=0)

    def up(x):
        return along(x, 4)

    def even(x):
        return lax.ppermute(x, "outer", [(i, i ^ 1) for i in ring])

    def odd(x):
        return lax.ppermute(x, "outer", [(i, i ^ 3) for i in ring])

    def corner(x):
        return lax.ppermute(x, "outer", [(i, (i + 7 - 2 * (i % 4)) % outer) for i in ring if i % 4 >= 2])

    A, B = 0, 1

    a0 = project_keys(0, runs, positions, normed, near, kv, cos, sin)[None]
    a1, e0, o0 = up(a0), even(a0), odd(a0)
    qa = project_queries(0, runs, positions, after(normed, a0), near, w_query, b_query, cos, sin)

    far_tokens = after(far_tokens, qa, a1, e0, o0)
    far_near = normalize(across(far_tokens, 1), norm_gain)
    far = normalize(far_tokens, norm_gain)
    b0 = project_keys(1, runs, positions, far, far_near, kv, cos, sin)[None]
    u0 = pack(a1, b0)
    u1, e1, o1 = up(u0), even(pack(u0, o0)), odd(u0)
    qb = project_queries(1, runs, positions, after(far, b0), far_near, w_query, b_query, cos, sin)
    came1 = ((A, "up", 1, a1, 0), (A, "even", 0, e0, 0), (A, "odd", 0, o0, 0))
    state = attend(B, came1, runs, positions, qb, own=(a0, b0))

    v1 = after(u1, state)
    u2, e2, o2 = up(v1), even(pack(v1, o1[1:2])), odd(pack(v1, e1[0:1]))
    came2 = ((A, "up", 2, u1, 0), (B, "up", 1, u1, 1), (A, "even", 1, e1, 0), (B, "even", 0, e1, 1),
             (A, "cross", 0, e1, 2), (A, "odd", 1, o1, 0), (B, "odd", 0, o1, 1))
    state = attend(B, came2, runs, positions, qb, state)
    near_state = attend(A, came1, runs, positions, after(qa, state), own=(a0, b0))

    v2 = after(u2, near_state)
    u3, e3, o3 = up(pack(v2[1:2], o2[2:3])), even(pack(v2, o2[1:2])), odd(v2)
    came3 = ((A, "up", 3, u2, 0), (B, "up", 2, u2, 1), (A, "even", 2, e2, 0), (B, "even", 1, e2, 1),
             (B, "cross", 0, e2, 2), (A, "odd", 2, o2, 0), (B, "odd", 1, o2, 1), (A, "cross", 1, o2, 2))
    state = attend(B, came3, runs, positions, qb, state)

    v3 = after(u3, state)
    u4, e4, o4 = up(pack(v3[1:2], o3[0:1])), even(pack(v3[0:1], o3[1:2])), odd(v3[0:1])
    c4 = corner(pack(v3[0:1], e3[1:2]))
    came4 = ((B, "up", 3, u3, 0), (A, "cross", 2, u3, 1), (A, "even", 3, e3, 0), (B, "even", 2, e3, 1),
             (B, "cross", 1, e3, 2), (A, "odd", 3, o3, 0), (B, "odd", 2, o3, 1))
    state = attend(B, came4, runs, positions, qb, state)
    near_state = attend(A, came2, runs, positions, after(qa, state), near_state)
    came5 = ((B, "even", 3, e4, 0), (B, "cross", 2, e4, 1), (B, "odd", 3, o4, 0), (A, "cross", 3, u4, 0),
             (A, "corner", 3, u4, 1), (B, "corner", 3, c4, 0), (B, "cross", 3, c4, 1))

    keep_far, send_far = attend_last(B, came5, runs, positions, after(qb, near_state), state, w_out)
    got_far = across(send_far, 1)
    other = (keep_far.astype(F32) + got_far.astype(F32)).astype(BF16)
    arrived = across(other, 2)
    keep_near, send_near = attend_last(
        A, came3 + came4 + came5, runs, positions, after(qa, other), near_state, w_out
    )
    got_near = across(send_near, 1)
    return (keep_near.astype(F32) + got_near.astype(F32) + arrived.astype(F32)).astype(BF16)


def solution(mesh):
    in_specs = (
        P(("outer", "inner"), None),
        P(),
        P(None, "inner"),
        P("inner"),
        P(None, "inner"),
        P("inner"),
        P(None, "inner"),
        P("inner"),
        P("inner", None),
        P(("outer", "inner")),
    )
    out_specs = P(("outer", "inner"), None)
    return jax.shard_map(local, mesh=mesh, in_specs=in_specs, out_specs=out_specs, check_vma=False)
```

```python
import functools

import jax
import jax.numpy as jnp
from jax import lax
from jax.experimental import pallas as pl
from jax.experimental.pallas import tpu as pltpu
from jax.sharding import PartitionSpec as P

HEAD_DIM = 128
VISITS = 14
HALF = 256
SHARD = 128
STRIP = 128
HEADS = 5
TILE = 16
MSG = HALF + HALF + TILE
STATE = HEAD_DIM + 16
PEAK, TOTAL = HEAD_DIM, HEAD_DIM + 8

rope_base = 10000000.0
norm_eps = 1e-06
masked_score = -1e30
EXP_SCALE = HEAD_DIM ** (-0.5) * 1.4426950408889634
F32, BF16 = jnp.float32, jnp.bfloat16
VMEM_BYTES = 24 * 2**20

WHOLE = pl.BlockSpec(memory_space=pltpu.VMEM)
SCALARS = pl.BlockSpec(memory_space=pltpu.SMEM)


def params():
    return pltpu.CompilerParams(vmem_limit_bytes=VMEM_BYTES)


def cost(flops, data, exps=0):
    return pl.CostEstimate(flops=flops, bytes_accessed=data, transcendentals=exps)


def where_am_i(pos_ref, runs):
    first = pos_ref[0]
    run = lax.shift_right_logical(first, 8)
    second = run >= runs // 2
    lead = jnp.where(second, runs - 1 - run, run)
    core = lax.bitwise_and(lax.shift_right_logical(first, 7), 1)
    return lead, jnp.where(second, 1, 0), core


def norm_kernel(tokens_ref, gain_ref, out_ref):
    values = tokens_ref[...].astype(F32)
    scale = lax.rsqrt(jnp.mean(values * values, axis=-1, keepdims=True) + norm_eps)
    out_ref[...] = (values * scale * gain_ref[...][None, :]).astype(BF16)


def normalize(tokens, gain):
    return pl.pallas_call(
        norm_kernel,
        out_shape=jax.ShapeDtypeStruct(tokens.shape, BF16),
        in_specs=[WHOLE, WHOLE],
        out_specs=WHOLE,
        compiler_params=params(),
        cost_estimate=cost(5 * tokens.size, 4 * tokens.size),
    )(tokens, gain)


def gather_rows(pos_ref, runs, own_ref, other_ref, rows):
    lead, _, core = where_am_i(pos_ref, runs)
    rows[pl.ds(pl.multiple_of(core * SHARD, SHARD), SHARD), :] = own_ref[...]
    rows[pl.ds(pl.multiple_of((1 - core) * SHARD, SHARD), SHARD), :] = other_ref[...]
    return lead


def rope_for(half, cos_ref, sin_ref):
    lane = lax.broadcasted_iota(jnp.int32, (HALF, HEAD_DIM), 1)
    mine = (lane < HEAD_DIM // 2) if half == 0 else (lane >= HEAD_DIM // 2)
    cos, sin = cos_ref[...], sin_ref[...]
    cos = jnp.where(mine, cos, pltpu.roll(cos, HEAD_DIM // 2, 1))
    sin = jnp.where(mine, sin, pltpu.roll(sin, HEAD_DIM // 2, 1))
    sin = jnp.where(lane < HEAD_DIM // 2, -sin, sin)
    return lambda u: u * cos + pltpu.roll(u, HEAD_DIM // 2, 1) * sin


def key_kernel(half, runs, pos_ref, own_ref, other_ref, wk_ref, wv_ref, bk_ref, bv_ref, cos_ref, sin_ref,
               msg_ref, rows):
    lead = gather_rows(pos_ref, runs, own_ref, other_ref, rows)
    x = rows[...]
    rope = rope_for(half, cos_ref, sin_ref)
    keys = jnp.dot(x, wk_ref[...], preferred_element_type=F32) + bk_ref[...][None, :]
    msg_ref[0:HALF, :] = rope(keys).astype(BF16)
    values = jnp.dot(x, wv_ref[...], preferred_element_type=F32) + bv_ref[...][None, :]
    flipped = values.T.astype(BF16)
    msg_ref[HALF:HALF + SHARD, :] = flipped[:, 0:SHARD]
    msg_ref[HALF + SHARD:2 * HALF, :] = flipped[:, SHARD:HALF]
    msg_ref[2 * HALF:MSG, :] = jnp.full((TILE, HEAD_DIM), lead.astype(F32), F32).astype(BF16)


def query_kernel(half, runs, pos_ref, own_ref, other_ref, wq_ref, bq_ref, cos_ref, sin_ref, q_ref, rows):
    gather_rows(pos_ref, runs, own_ref, other_ref, rows)
    x = rows[...]
    rope = rope_for(half, cos_ref, sin_ref)
    for h in range(HEADS):
        cols = slice(h * HEAD_DIM, (h + 1) * HEAD_DIM)
        heads = jnp.dot(x, wq_ref[:, cols], preferred_element_type=F32) + bq_ref[cols][None, :]
        q_ref[:, h * HALF:(h + 1) * HALF] = rope(heads).T.astype(BF16)


def project_keys(half, runs, positions, own, other, weights, cos, sin):
    features = own.shape[1]
    return pl.pallas_call(
        functools.partial(key_kernel, half, runs),
        out_shape=jax.ShapeDtypeStruct((MSG, HEAD_DIM), BF16),
        in_specs=[SCALARS] + [WHOLE] * 8,
        out_specs=WHOLE,
        scratch_shapes=[pltpu.VMEM((HALF, features), BF16)],
        compiler_params=params(),
        cost_estimate=cost(4 * HALF * features * HEAD_DIM, 4 * features * HEAD_DIM),
    )(positions, own, other, *weights, cos, sin)


def project_queries(half, runs, positions, own, other, w_query, b_query, cos, sin):
    features = own.shape[1]
    return pl.pallas_call(
        functools.partial(query_kernel, half, runs),
        out_shape=jax.ShapeDtypeStruct((HEAD_DIM, HEADS * HALF), BF16),
        in_specs=[SCALARS] + [WHOLE] * 6,
        out_specs=WHOLE,
        scratch_shapes=[pltpu.VMEM((HALF, features), BF16)],
        compiler_params=params(),
        cost_estimate=cost(2 * HALF * features * HEADS * HEAD_DIM, 2 * features * HEADS * HEAD_DIM),
    )(positions, own, other, w_query, b_query, cos, sin)


def distance(kind, level, column):
    if kind == "up":
        return 4 * level + 0 * column
    if kind == "even":
        return 4 * level + column - lax.bitwise_xor(column, 1)
    if kind == "odd":
        return 4 * level + 2 * column - 3
    if kind == "cross":
        return 4 * level + jnp.where(column < 2, -2, 2)
    return jnp.where(column == 0, VISITS - 1, 0)


def visit(q_ref, msgs, state, at, first=False):
    k = msgs[at, 0:HALF, :]
    vt = jnp.concatenate([msgs[at, HALF:HALF + SHARD, :], msgs[at, HALF + SHARD:2 * HALF, :]], axis=1)
    for strip in range(HEADS * HALF // STRIP):
        cols = slice(strip * STRIP, (strip + 1) * STRIP)
        s = jnp.dot(k, q_ref[:, cols], preferred_element_type=F32)
        if first:
            key_at = lax.broadcasted_iota(jnp.int32, s.shape, 0)
            row_at = lax.broadcasted_iota(jnp.int32, s.shape, 1) + strip * STRIP % HALF
            s = jnp.where(key_at <= row_at, s, masked_score)
            peak = jnp.max(s, axis=0, keepdims=True)
        else:
            old = state[PEAK:PEAK + 1, cols]
            peak = jnp.maximum(old, jnp.max(s, axis=0, keepdims=True))
            factor = jnp.exp2((old - peak) * EXP_SCALE)
        expo = jnp.exp2((s - peak) * EXP_SCALE)
        total = jnp.sum(expo, axis=0, keepdims=True)
        mixed = jnp.dot(vt, expo.astype(BF16), preferred_element_type=F32)
        if not first:
            total = total + state[TOTAL:TOTAL + 1, cols] * factor
            mixed = mixed + state[0:HEAD_DIM, cols] * factor
        state[PEAK:PEAK + 1, cols] = peak
        state[TOTAL:TOTAL + 1, cols] = total
        state[0:HEAD_DIM, cols] = mixed


def attend_all(target, specs, places, arrays, pos_ref, runs, q_ref, msgs, state, todo, own=(), paired=False):
    lead, second, _ = where_am_i(pos_ref, runs)
    column = lax.bitwise_and(pos_ref[SHARD], 3)
    todo[0] = 0
    wanted = []
    for (half, kind, level), (which, index) in zip(specs, places):
        back = distance(kind, level, column)
        valid = jnp.logical_and(back >= 1, back <= VISITS - 1)
        role = second if half == 0 else 1 - second
        if half == target:
            run = jnp.max(arrays[which][index, 2 * HALF:MSG, :].astype(F32)).astype(jnp.int32)
            seen = jnp.where(role == 0, run < lead, run > lead)
        else:
            seen = role == 0
        wanted.append(jnp.logical_and(valid, seen))
    sources = [(arrays[which], index) for which, index in places]
    if own:
        msgs[0, :, :] = own[target][0, :, :]
        visit(q_ref, msgs, state, 0, True)
        wanted.append(second == 1 - target)
        sources.append((own[1 - target], 0))
    for want, (ref, index) in zip(wanted, sources):
        @pl.when(want)
        def _(ref=ref, index=index):
            place = todo[0]
            msgs[place, :, :] = ref[index, :, :]
            todo[0] = place + 1

    count = todo[0]

    def one(i, carry):
        visit(q_ref, msgs, state, i)
        return carry

    def two(i, carry):
        visit(q_ref, msgs, state, 2 * i)
        visit(q_ref, msgs, state, 2 * i + 1)
        return carry

    if paired:
        lax.fori_loop(0, lax.shift_right_logical(count, 1), two, 0)

        @pl.when(lax.bitwise_and(count, 1) == 1)
        def _():
            visit(q_ref, msgs, state, count - 1)
    else:
        lax.fori_loop(0, count, one, 0)


def attend_kernel(target, specs, places, own, runs, pos_ref, q_ref, *rest):
    state, msgs, todo = rest[-3:]
    if own:
        attend_all(target, specs, places, rest[2:-3], pos_ref, runs, q_ref, msgs, state, todo, own=rest[:2])
    else:
        state[...] = rest[0][...]
        attend_all(target, specs, places, rest[1:-3], pos_ref, runs, q_ref, msgs, state, todo)


def unpack(messages):
    arrays, places, specs = [], [], []
    for half, kind, level, array, at in messages:
        for i, known in enumerate(arrays):
            if known is array:
                break
        else:
            i = len(arrays)
            arrays.append(array)
        places.append((i, at))
        specs.append((half, kind, level))
    return tuple(specs), tuple(places), arrays


def working(count):
    return [pltpu.VMEM((count, MSG, HEAD_DIM), BF16), pltpu.SMEM((1,), jnp.int32)]


def task_cost(count, more=0):
    return cost(count * 2 * HEADS * HALF * HALF * HEAD_DIM + more, 2**21, count * HEADS * HALF * HALF // 2)


def attend(target, messages, runs, positions, q, state=None, own=()):
    specs, places, arrays = unpack(messages)
    before = list(own) if own else [state]
    return pl.pallas_call(
        functools.partial(attend_kernel, target, specs, places, bool(own), runs),
        out_shape=jax.ShapeDtypeStruct((STATE, HEADS * HALF), F32),
        in_specs=[SCALARS] + [WHOLE] * (1 + len(before) + len(arrays)),
        out_specs=WHOLE,
        scratch_shapes=working(len(specs) + 1),
        compiler_params=params(),
        cost_estimate=task_cost(len(specs)),
    )(positions, q, *before, *arrays)


def project_out(pos_ref, runs, mixed, w_ref, keep_ref, send_ref):
    _, _, core = where_am_i(pos_ref, runs)
    keep_at = pl.ds(pl.multiple_of(core * SHARD, SHARD), SHARD)
    send_at = pl.ds(pl.multiple_of((1 - core) * SHARD, SHARD), SHARD)
    x = jnp.concatenate([mixed[send_at, :], mixed[keep_at, :]], axis=0)
    width = 512
    for j in range(w_ref.shape[1] // width):
        cols = slice(j * width, (j + 1) * width)
        part = jnp.dot(x, w_ref[:, cols], preferred_element_type=F32).astype(BF16)
        send_ref[:, cols] = part[0:SHARD]
        keep_ref[:, cols] = part[SHARD:HALF]


def last_kernel(target, specs, places, runs, pos_ref, q_ref, state_in, w_ref, *rest):
    keep_ref, send_ref, msgs, todo, state, mixed = rest[-6:]
    state[...] = state_in[...]
    attend_all(target, specs, places, rest[:-6], pos_ref, runs, q_ref, msgs, state, todo, paired=target == 0)
    for h in range(HEADS):
        cols = slice(h * HALF, (h + 1) * HALF)
        scale = 1.0 / state[TOTAL:TOTAL + 1, cols]
        mixed[:, h * HEAD_DIM:(h + 1) * HEAD_DIM] = (state[0:HEAD_DIM, cols] * scale).T.astype(BF16)
    project_out(pos_ref, runs, mixed, w_ref, keep_ref, send_ref)


def attend_last(target, messages, runs, positions, q, state, w_out):
    specs, places, arrays = unpack(messages)
    part = jax.ShapeDtypeStruct((SHARD, w_out.shape[1]), BF16)
    return pl.pallas_call(
        functools.partial(last_kernel, target, specs, places, runs),
        out_shape=(part, part),
        in_specs=[SCALARS] + [WHOLE] * (3 + len(arrays)),
        out_specs=(WHOLE, WHOLE),
        scratch_shapes=working(len(specs)) + [pltpu.VMEM(state.shape, F32), pltpu.VMEM((HALF, HEADS * HEAD_DIM), BF16)],
        compiler_params=params(),
        cost_estimate=task_cost(len(specs), 2 * HALF * w_out.size),
    )(positions, q, state, w_out, *arrays)


def after(x, *earlier):
    return lax.optimization_barrier((x, *earlier))[0]


def local(tokens, norm_gain, w_query, b_query, w_key, b_key, w_value, b_value, w_out, positions):
    outer = lax.axis_size("outer")
    runs = 2 * outer

    def along(x, distance):
        return lax.ppermute(x, "outer", [(i, (i + distance) % outer) for i in range(outer)])

    def across(x, flip):
        return lax.ppermute(x, "inner", [(i, i ^ flip) for i in range(4)])

    far_tokens = across(tokens, 2)
    normed = normalize(tokens, norm_gain)
    near = across(normed, 1)

    run = positions[0] // HALF
    positions = jnp.concatenate([positions, lax.axis_index("outer")[None]])
    row = jnp.arange(HALF, dtype=jnp.int32)[:, None]
    lane = jnp.arange(HEAD_DIM, dtype=jnp.int32)[None, :]
    places = jnp.where(lane < HEAD_DIM // 2, run, runs - 1 - run) * HALF + row
    inverse = rope_base ** (-(jnp.arange(HEAD_DIM // 2, dtype=F32) * 2.0 / HEAD_DIM))
    angles = places.astype(F32) * jnp.concatenate([inverse, inverse])[None, :]
    cos, sin = jnp.cos(angles), jnp.sin(angles)

    kv = (w_key, w_value, b_key, b_value)
    ring = range(outer)

    def pack(*parts):
        return jnp.concatenate(parts, axis=0)

    def up(x):
        return along(x, 4)

    def even(x):
        return lax.ppermute(x, "outer", [(i, i ^ 1) for i in ring])

    def odd(x):
        return lax.ppermute(x, "outer", [(i, i ^ 3) for i in ring])

    def corner(x):
        return lax.ppermute(x, "outer", [(i, (i + 7 - 2 * (i % 4)) % outer) for i in ring if i % 4 >= 2])

    A, B = 0, 1

    a0 = project_keys(0, runs, positions, normed, near, kv, cos, sin)[None]
    a1, e0, o0 = up(a0), even(a0), odd(a0)
    qa = project_queries(0, runs, positions, after(normed, a0), near, w_query, b_query, cos, sin)

    far_tokens = after(far_tokens, qa, a1, e0, o0)
    far_near = normalize(across(far_tokens, 1), norm_gain)
    far = normalize(far_tokens, norm_gain)
    b0 = project_keys(1, runs, positions, far, far_near, kv, cos, sin)[None]
    u0 = pack(a1, b0)
    u1, e1, o1 = up(u0), even(pack(u0, o0)), odd(u0)
    qb = project_queries(1, runs, positions, after(far, b0), far_near, w_query, b_query, cos, sin)
    came1 = ((A, "up", 1, a1, 0), (A, "even", 0, e0, 0), (A, "odd", 0, o0, 0))
    state = attend(B, came1, runs, positions, qb, own=(a0, b0))

    v1 = after(u1, state)
    u2, e2, o2 = up(v1), even(pack(v1, o1[1:2])), odd(pack(v1, e1[0:1]))
    came2 = ((A, "up", 2, u1, 0), (B, "up", 1, u1, 1), (A, "even", 1, e1, 0), (B, "even", 0, e1, 1),
             (A, "cross", 0, e1, 2), (A, "odd", 1, o1, 0), (B, "odd", 0, o1, 1))
    state = attend(B, came2, runs, positions, qb, state)
    near_state = attend(A, came1, runs, positions, after(qa, state), own=(a0, b0))

    v2 = after(u2, near_state)
    u3, e3, o3 = up(pack(v2[1:2], o2[2:3])), even(pack(v2, o2[1:2])), odd(v2)
    came3 = ((A, "up", 3, u2, 0), (B, "up", 2, u2, 1), (A, "even", 2, e2, 0), (B, "even", 1, e2, 1),
             (B, "cross", 0, e2, 2), (A, "odd", 2, o2, 0), (B, "odd", 1, o2, 1), (A, "cross", 1, o2, 2))
    state = attend(B, came3, runs, positions, qb, state)

    v3 = after(u3, state)
    u4, e4, o4 = up(pack(v3[1:2], o3[0:1])), even(pack(v3[0:1], o3[1:2])), odd(v3[0:1])
    c4 = corner(pack(v3[0:1], e3[1:2]))
    came4 = ((B, "up", 3, u3, 0), (A, "cross", 2, u3, 1), (A, "even", 3, e3, 0), (B, "even", 2, e3, 1),
             (B, "cross", 1, e3, 2), (A, "odd", 3, o3, 0), (B, "odd", 2, o3, 1))
    state = attend(B, came4, runs, positions, qb, state)
    near_state = attend(A, came2, runs, positions, after(qa, state), near_state)
    came5 = ((B, "even", 3, e4, 0), (B, "cross", 2, e4, 1), (B, "odd", 3, o4, 0), (A, "cross", 3, u4, 0),
             (A, "corner", 3, u4, 1), (B, "corner", 3, c4, 0), (B, "cross", 3, c4, 1))

    keep_far, send_far = attend_last(B, came5, runs, positions, after(qb, near_state), state, w_out)
    got_far = across(send_far, 1)
    other = (keep_far.astype(F32) + got_far.astype(F32)).astype(BF16)
    arrived = across(other, 2)
    keep_near, send_near = attend_last(
        A, came3 + came4 + came5, runs, positions, after(qa, other), near_state, w_out
    )
    got_near = across(send_near, 1)
    return (keep_near.astype(F32) + got_near.astype(F32) + arrived.astype(F32)).astype(BF16)


def solution(mesh):
    in_specs = (
        P(("outer", "inner"), None),
        P(),
        P(None, "inner"),
        P("inner"),
        P(None, "inner"),
        P("inner"),
        P(None, "inner"),
        P("inner"),
        P("inner", None),
        P(("outer", "inner")),
    )
    out_specs = P(("outer", "inner"), None)
    return jax.shard_map(local, mesh=mesh, in_specs=in_specs, out_specs=out_specs, check_vma=False)
```

```python
import functools

import jax
import jax.numpy as jnp
from jax import lax
from jax.experimental import pallas as pl
from jax.experimental.pallas import tpu as pltpu
from jax.sharding import PartitionSpec as P

HEAD_DIM = 128
VISITS = 14
HALF = 256
SHARD = 128
STRIP = 128
HEADS = 5
TILE = 16
MSG = HALF + HALF + TILE
STATE = HEAD_DIM + 16
PEAK, TOTAL = HEAD_DIM, HEAD_DIM + 8

rope_base = 10000000.0
norm_eps = 1e-06
masked_score = -1e30
EXP_SCALE = HEAD_DIM ** (-0.5) * 1.4426950408889634
F32, BF16 = jnp.float32, jnp.bfloat16
VMEM_BYTES = 24 * 2**20

WHOLE = pl.BlockSpec(memory_space=pltpu.VMEM)
SCALARS = pl.BlockSpec(memory_space=pltpu.SMEM)


def params():
    return pltpu.CompilerParams(vmem_limit_bytes=VMEM_BYTES)


def cost(flops, data, exps=0):
    return pl.CostEstimate(flops=flops, bytes_accessed=data, transcendentals=exps)


def where_am_i(pos_ref, runs):
    first = pos_ref[0]
    run = lax.shift_right_logical(first, 8)
    second = run >= runs // 2
    lead = jnp.where(second, runs - 1 - run, run)
    core = lax.bitwise_and(lax.shift_right_logical(first, 7), 1)
    return lead, jnp.where(second, 1, 0), core


def norm_kernel(tokens_ref, gain_ref, out_ref):
    values = tokens_ref[...].astype(F32)
    scale = lax.rsqrt(jnp.mean(values * values, axis=-1, keepdims=True) + norm_eps)
    out_ref[...] = (values * scale * gain_ref[...][None, :]).astype(BF16)


def normalize(tokens, gain):
    return pl.pallas_call(
        norm_kernel,
        out_shape=jax.ShapeDtypeStruct(tokens.shape, BF16),
        in_specs=[WHOLE, WHOLE],
        out_specs=WHOLE,
        compiler_params=params(),
        cost_estimate=cost(5 * tokens.size, 4 * tokens.size),
    )(tokens, gain)


def gather_rows(pos_ref, runs, own_ref, other_ref, rows):
    lead, _, core = where_am_i(pos_ref, runs)
    rows[pl.ds(pl.multiple_of(core * SHARD, SHARD), SHARD), :] = own_ref[...]
    rows[pl.ds(pl.multiple_of((1 - core) * SHARD, SHARD), SHARD), :] = other_ref[...]
    return lead


def rope_for(half, cos_ref, sin_ref):
    lane = lax.broadcasted_iota(jnp.int32, (HALF, HEAD_DIM), 1)
    mine = (lane < HEAD_DIM // 2) if half == 0 else (lane >= HEAD_DIM // 2)
    cos, sin = cos_ref[...], sin_ref[...]
    cos = jnp.where(mine, cos, pltpu.roll(cos, HEAD_DIM // 2, 1))
    sin = jnp.where(mine, sin, pltpu.roll(sin, HEAD_DIM // 2, 1))
    sin = jnp.where(lane < HEAD_DIM // 2, -sin, sin)
    return lambda u: u * cos + pltpu.roll(u, HEAD_DIM // 2, 1) * sin


def key_kernel(half, runs, pos_ref, own_ref, other_ref, wk_ref, wv_ref, bk_ref, bv_ref, cos_ref, sin_ref,
               msg_ref, rows):
    lead = gather_rows(pos_ref, runs, own_ref, other_ref, rows)
    x = rows[...]
    rope = rope_for(half, cos_ref, sin_ref)
    keys = jnp.dot(x, wk_ref[...], preferred_element_type=F32) + bk_ref[...][None, :]
    msg_ref[0:HALF, :] = rope(keys).astype(BF16)
    values = jnp.dot(x, wv_ref[...], preferred_element_type=F32) + bv_ref[...][None, :]
    flipped = values.T.astype(BF16)
    msg_ref[HALF:HALF + SHARD, :] = flipped[:, 0:SHARD]
    msg_ref[HALF + SHARD:2 * HALF, :] = flipped[:, SHARD:HALF]
    msg_ref[2 * HALF:MSG, :] = jnp.full((TILE, HEAD_DIM), lead.astype(F32), F32).astype(BF16)


def query_kernel(half, runs, pos_ref, own_ref, other_ref, wq_ref, bq_ref, cos_ref, sin_ref, q_ref, rows):
    gather_rows(pos_ref, runs, own_ref, other_ref, rows)
    x = rows[...]
    rope = rope_for(half, cos_ref, sin_ref)
    for h in range(HEADS):
        cols = slice(h * HEAD_DIM, (h + 1) * HEAD_DIM)
        heads = jnp.dot(x, wq_ref[:, cols], preferred_element_type=F32) + bq_ref[cols][None, :]
        q_ref[:, h * HALF:(h + 1) * HALF] = rope(heads).T.astype(BF16)


def project_keys(half, runs, positions, own, other, weights, cos, sin):
    features = own.shape[1]
    return pl.pallas_call(
        functools.partial(key_kernel, half, runs),
        out_shape=jax.ShapeDtypeStruct((MSG, HEAD_DIM), BF16),
        in_specs=[SCALARS] + [WHOLE] * 8,
        out_specs=WHOLE,
        scratch_shapes=[pltpu.VMEM((HALF, features), BF16)],
        compiler_params=params(),
        cost_estimate=cost(4 * HALF * features * HEAD_DIM, 4 * features * HEAD_DIM),
    )(positions, own, other, *weights, cos, sin)


def project_queries(half, runs, positions, own, other, w_query, b_query, cos, sin):
    features = own.shape[1]
    return pl.pallas_call(
        functools.partial(query_kernel, half, runs),
        out_shape=jax.ShapeDtypeStruct((HEAD_DIM, HEADS * HALF), BF16),
        in_specs=[SCALARS] + [WHOLE] * 6,
        out_specs=WHOLE,
        scratch_shapes=[pltpu.VMEM((HALF, features), BF16)],
        compiler_params=params(),
        cost_estimate=cost(2 * HALF * features * HEADS * HEAD_DIM, 2 * features * HEADS * HEAD_DIM),
    )(positions, own, other, w_query, b_query, cos, sin)


def distance(kind, level, column):
    if kind == "up":
        return 4 * level + 0 * column
    if kind == "even":
        return 4 * level + column - lax.bitwise_xor(column, 1)
    if kind == "odd":
        return 4 * level + 2 * column - 3
    if kind == "cross":
        return 4 * level + jnp.where(column < 2, -2, 2)
    return jnp.where(column == 0, VISITS - 1, 0)


def visit(q_ref, msgs, state, at, first=False):
    k = msgs[at, 0:HALF, :]
    vt = jnp.concatenate([msgs[at, HALF:HALF + SHARD, :], msgs[at, HALF + SHARD:2 * HALF, :]], axis=1)
    for strip in range(HEADS * HALF // STRIP):
        cols = slice(strip * STRIP, (strip + 1) * STRIP)
        s = jnp.dot(k, q_ref[:, cols], preferred_element_type=F32)
        if first:
            key_at = lax.broadcasted_iota(jnp.int32, s.shape, 0)
            row_at = lax.broadcasted_iota(jnp.int32, s.shape, 1) + strip * STRIP % HALF
            s = jnp.where(key_at <= row_at, s, masked_score)
            peak = jnp.max(s, axis=0, keepdims=True)
        else:
            old = state[PEAK:PEAK + 1, cols]
            peak = jnp.maximum(old, jnp.max(s, axis=0, keepdims=True))
            factor = jnp.exp2((old - peak) * EXP_SCALE)
        expo = jnp.exp2((s - peak) * EXP_SCALE)
        total = jnp.sum(expo, axis=0, keepdims=True)
        mixed = jnp.dot(vt, expo.astype(BF16), preferred_element_type=F32)
        if not first:
            total = total + state[TOTAL:TOTAL + 1, cols] * factor
            mixed = mixed + state[0:HEAD_DIM, cols] * factor
        state[PEAK:PEAK + 1, cols] = peak
        state[TOTAL:TOTAL + 1, cols] = total
        state[0:HEAD_DIM, cols] = mixed


def attend_all(target, specs, places, arrays, pos_ref, runs, q_ref, msgs, state, todo, own=(), paired=False):
    lead, second, _ = where_am_i(pos_ref, runs)
    column = lax.bitwise_and(pos_ref[SHARD], 3)
    todo[0] = 0
    wanted = []
    for (half, kind, level), (which, index) in zip(specs, places):
        back = distance(kind, level, column)
        valid = jnp.logical_and(back >= 1, back <= VISITS - 1)
        role = second if half == 0 else 1 - second
        if half == target:
            run = jnp.max(arrays[which][index, 2 * HALF:MSG, :].astype(F32)).astype(jnp.int32)
            seen = jnp.where(role == 0, run < lead, run > lead)
        else:
            seen = role == 0
        wanted.append(jnp.logical_and(valid, seen))
    sources = [(arrays[which], index) for which, index in places]
    if own:
        msgs[0, :, :] = own[target][0, :, :]
        visit(q_ref, msgs, state, 0, True)
        wanted.append(second == 1 - target)
        sources.append((own[1 - target], 0))
    for want, (ref, index) in zip(wanted, sources):
        @pl.when(want)
        def _(ref=ref, index=index):
            place = todo[0]
            msgs[place, :, :] = ref[index, :, :]
            todo[0] = place + 1

    count = todo[0]

    def one(i, carry):
        visit(q_ref, msgs, state, i)
        return carry

    def two(i, carry):
        visit(q_ref, msgs, state, 2 * i)
        visit(q_ref, msgs, state, 2 * i + 1)
        return carry

    if paired:
        lax.fori_loop(0, lax.shift_right_logical(count, 1), two, 0)

        @pl.when(lax.bitwise_and(count, 1) == 1)
        def _():
            visit(q_ref, msgs, state, count - 1)
    else:
        lax.fori_loop(0, count, one, 0)


def attend_kernel(target, specs, places, own, paired, runs, pos_ref, q_ref, *rest):
    state, msgs, todo = rest[-3:]
    if own:
        attend_all(target, specs, places, rest[2:-3], pos_ref, runs, q_ref, msgs, state, todo, own=rest[:2])
    else:
        state[...] = rest[0][...]
        attend_all(target, specs, places, rest[1:-3], pos_ref, runs, q_ref, msgs, state, todo, paired=paired)


def unpack(messages):
    arrays, places, specs = [], [], []
    for half, kind, level, array, at in messages:
        for i, known in enumerate(arrays):
            if known is array:
                break
        else:
            i = len(arrays)
            arrays.append(array)
        places.append((i, at))
        specs.append((half, kind, level))
    return tuple(specs), tuple(places), arrays


def working(count):
    return [pltpu.VMEM((count, MSG, HEAD_DIM), BF16), pltpu.SMEM((1,), jnp.int32)]


def task_cost(count, more=0):
    return cost(count * 2 * HEADS * HALF * HALF * HEAD_DIM + more, 2**21, count * HEADS * HALF * HALF // 2)


def attend(target, messages, runs, positions, q, state=None, own=(), paired=False):
    specs, places, arrays = unpack(messages)
    before = list(own) if own else [state]
    return pl.pallas_call(
        functools.partial(attend_kernel, target, specs, places, bool(own), paired, runs),
        out_shape=jax.ShapeDtypeStruct((STATE, HEADS * HALF), F32),
        in_specs=[SCALARS] + [WHOLE] * (1 + len(before) + len(arrays)),
        out_specs=WHOLE,
        scratch_shapes=working(len(specs) + 1),
        compiler_params=params(),
        cost_estimate=task_cost(len(specs)),
    )(positions, q, *before, *arrays)


def project_out(pos_ref, runs, mixed, w_ref, keep_ref, send_ref):
    _, _, core = where_am_i(pos_ref, runs)
    keep_at = pl.ds(pl.multiple_of(core * SHARD, SHARD), SHARD)
    send_at = pl.ds(pl.multiple_of((1 - core) * SHARD, SHARD), SHARD)
    x = jnp.concatenate([mixed[send_at, :], mixed[keep_at, :]], axis=0)
    width = 512
    for j in range(w_ref.shape[1] // width):
        cols = slice(j * width, (j + 1) * width)
        part = jnp.dot(x, w_ref[:, cols], preferred_element_type=F32).astype(BF16)
        send_ref[:, cols] = part[0:SHARD]
        keep_ref[:, cols] = part[SHARD:HALF]


def last_kernel(target, specs, places, runs, pos_ref, q_ref, state_in, w_ref, *rest):
    keep_ref, send_ref, msgs, todo, state, mixed = rest[-6:]
    state[...] = state_in[...]
    attend_all(target, specs, places, rest[:-6], pos_ref, runs, q_ref, msgs, state, todo, paired=True)
    for h in range(HEADS):
        cols = slice(h * HALF, (h + 1) * HALF)
        scale = 1.0 / state[TOTAL:TOTAL + 1, cols]
        mixed[:, h * HEAD_DIM:(h + 1) * HEAD_DIM] = (state[0:HEAD_DIM, cols] * scale).T.astype(BF16)
    project_out(pos_ref, runs, mixed, w_ref, keep_ref, send_ref)


def attend_last(target, messages, runs, positions, q, state, w_out):
    specs, places, arrays = unpack(messages)
    part = jax.ShapeDtypeStruct((SHARD, w_out.shape[1]), BF16)
    return pl.pallas_call(
        functools.partial(last_kernel, target, specs, places, runs),
        out_shape=(part, part),
        in_specs=[SCALARS] + [WHOLE] * (3 + len(arrays)),
        out_specs=(WHOLE, WHOLE),
        scratch_shapes=working(len(specs)) + [pltpu.VMEM(state.shape, F32), pltpu.VMEM((HALF, HEADS * HEAD_DIM), BF16)],
        compiler_params=params(),
        cost_estimate=task_cost(len(specs), 2 * HALF * w_out.size),
    )(positions, q, state, w_out, *arrays)


def after(x, *earlier):
    return lax.optimization_barrier((x, *earlier))[0]


def local(tokens, norm_gain, w_query, b_query, w_key, b_key, w_value, b_value, w_out, positions):
    outer = lax.axis_size("outer")
    runs = 2 * outer

    def along(x, distance):
        return lax.ppermute(x, "outer", [(i, (i + distance) % outer) for i in range(outer)])

    def across(x, flip):
        return lax.ppermute(x, "inner", [(i, i ^ flip) for i in range(4)])

    far_tokens = across(tokens, 2)
    normed = normalize(tokens, norm_gain)
    near = across(normed, 1)

    run = positions[0] // HALF
    positions = jnp.concatenate([positions, lax.axis_index("outer")[None]])
    row = jnp.arange(HALF, dtype=jnp.int32)[:, None]
    lane = jnp.arange(HEAD_DIM, dtype=jnp.int32)[None, :]
    places = jnp.where(lane < HEAD_DIM // 2, run, runs - 1 - run) * HALF + row
    inverse = rope_base ** (-(jnp.arange(HEAD_DIM // 2, dtype=F32) * 2.0 / HEAD_DIM))
    angles = places.astype(F32) * jnp.concatenate([inverse, inverse])[None, :]
    cos, sin = jnp.cos(angles), jnp.sin(angles)

    kv = (w_key, w_value, b_key, b_value)
    ring = range(outer)

    def pack(*parts):
        return jnp.concatenate(parts, axis=0)

    def up(x):
        return along(x, 4)

    def even(x):
        return lax.ppermute(x, "outer", [(i, i ^ 1) for i in ring])

    def odd(x):
        return lax.ppermute(x, "outer", [(i, i ^ 3) for i in ring])

    def corner(x):
        return lax.ppermute(x, "outer", [(i, (i + 7 - 2 * (i % 4)) % outer) for i in ring if i % 4 >= 2])

    A, B = 0, 1

    a0 = project_keys(0, runs, positions, normed, near, kv, cos, sin)[None]
    a1, e0, o0 = up(a0), even(a0), odd(a0)
    qa = project_queries(0, runs, positions, after(normed, a0), near, w_query, b_query, cos, sin)

    far_tokens = after(far_tokens, qa, a1, e0, o0)
    far_near = normalize(across(far_tokens, 1), norm_gain)
    far = normalize(far_tokens, norm_gain)
    b0 = project_keys(1, runs, positions, far, far_near, kv, cos, sin)[None]
    u0 = pack(a1, b0)
    u1, e1, o1 = up(u0), even(pack(u0, o0)), odd(u0)
    qb = project_queries(1, runs, positions, after(far, b0), far_near, w_query, b_query, cos, sin)
    came1 = ((A, "up", 1, a1, 0), (A, "even", 0, e0, 0), (A, "odd", 0, o0, 0))
    state = attend(B, came1, runs, positions, qb, own=(a0, b0))

    v1 = after(u1, state)
    u2, e2, o2 = up(v1), even(pack(v1, o1[1:2])), odd(pack(v1, e1[0:1]))
    came2 = ((A, "up", 2, u1, 0), (B, "up", 1, u1, 1), (A, "even", 1, e1, 0), (B, "even", 0, e1, 1),
             (A, "cross", 0, e1, 2), (A, "odd", 1, o1, 0), (B, "odd", 0, o1, 1))
    state = attend(B, came2, runs, positions, qb, state)
    near_state = attend(A, came1, runs, positions, after(qa, state), own=(a0, b0))

    v2 = after(u2, near_state)
    u3, e3, o3 = up(pack(v2[1:2], o2[2:3])), even(pack(v2, o2[1:2])), odd(after(v2, e2, o2))
    came3 = ((A, "up", 3, u2, 0), (B, "up", 2, u2, 1), (A, "even", 2, e2, 0), (B, "even", 1, e2, 1),
             (B, "cross", 0, e2, 2), (A, "odd", 2, o2, 0), (B, "odd", 1, o2, 1), (A, "cross", 1, o2, 2))
    state = attend(B, came3, runs, positions, qb, state, paired=True)

    v3 = after(u3, state)
    u4, e4, o4 = up(pack(v3[1:2], o3[0:1])), even(pack(v3[0:1], o3[1:2])), odd(v3[0:1])
    c4 = corner(pack(v3[0:1], e3[1:2]))
    came4 = ((B, "up", 3, u3, 0), (A, "cross", 2, u3, 1), (A, "even", 3, e3, 0), (B, "even", 2, e3, 1),
             (B, "cross", 1, e3, 2), (A, "odd", 3, o3, 0), (B, "odd", 2, o3, 1))
    state = attend(B, came4, runs, positions, qb, state)
    near_state = attend(A, came2, runs, positions, after(qa, state), near_state)
    came5 = ((B, "even", 3, e4, 0), (B, "cross", 2, e4, 1), (B, "odd", 3, o4, 0), (A, "cross", 3, u4, 0),
             (A, "corner", 3, u4, 1), (B, "corner", 3, c4, 0), (B, "cross", 3, c4, 1))

    keep_far, send_far = attend_last(B, came5, runs, positions, after(qb, near_state), state, w_out)
    got_far = across(send_far, 1)
    other = (keep_far.astype(F32) + got_far.astype(F32)).astype(BF16)
    arrived = across(other, 2)
    keep_near, send_near = attend_last(
        A, came3 + came4 + came5, runs, positions, after(qa, other), near_state, w_out
    )
    got_near = across(send_near, 1)
    return (keep_near.astype(F32) + got_near.astype(F32) + arrived.astype(F32)).astype(BF16)


def solution(mesh):
    in_specs = (
        P(("outer", "inner"), None),
        P(),
        P(None, "inner"),
        P("inner"),
        P(None, "inner"),
        P("inner"),
        P(None, "inner"),
        P("inner"),
        P("inner", None),
        P(("outer", "inner")),
    )
    out_specs = P(("outer", "inner"), None)
    return jax.shard_map(local, mesh=mesh, in_specs=in_specs, out_specs=out_specs, check_vma=False)
```

```python
import functools

import jax
import jax.numpy as jnp
from jax import lax
from jax.experimental import pallas as pl
from jax.experimental.pallas import tpu as pltpu
from jax.sharding import PartitionSpec as P

HEAD_DIM = 128
VISITS = 14
HALF = 256
SHARD = 128
STRIP = 128
HEADS = 5
TILE = 16
MSG = HALF + HALF + TILE
STATE = HEAD_DIM + 16
PEAK, TOTAL = HEAD_DIM, HEAD_DIM + 8

rope_base = 10000000.0
norm_eps = 1e-06
masked_score = -1e30
EXP_SCALE = HEAD_DIM ** (-0.5) * 1.4426950408889634
F32, BF16 = jnp.float32, jnp.bfloat16
VMEM_BYTES = 24 * 2**20

WHOLE = pl.BlockSpec(memory_space=pltpu.VMEM)
SCALARS = pl.BlockSpec(memory_space=pltpu.SMEM)


def params():
    return pltpu.CompilerParams(vmem_limit_bytes=VMEM_BYTES)


def cost(flops, data, exps=0):
    return pl.CostEstimate(flops=flops, bytes_accessed=data, transcendentals=exps)


def where_am_i(pos_ref, runs):
    first = pos_ref[0]
    run = lax.shift_right_logical(first, 8)
    second = run >= runs // 2
    lead = jnp.where(second, runs - 1 - run, run)
    core = lax.bitwise_and(lax.shift_right_logical(first, 7), 1)
    return lead, jnp.where(second, 1, 0), core


def norm_kernel(tokens_ref, gain_ref, out_ref):
    values = tokens_ref[...].astype(F32)
    scale = lax.rsqrt(jnp.mean(values * values, axis=-1, keepdims=True) + norm_eps)
    out_ref[...] = (values * scale * gain_ref[...][None, :]).astype(BF16)


def normalize(tokens, gain):
    return pl.pallas_call(
        norm_kernel,
        out_shape=jax.ShapeDtypeStruct(tokens.shape, BF16),
        in_specs=[WHOLE, WHOLE],
        out_specs=WHOLE,
        compiler_params=params(),
        cost_estimate=cost(5 * tokens.size, 4 * tokens.size),
    )(tokens, gain)


def gather_rows(pos_ref, runs, own_ref, other_ref, rows):
    lead, _, core = where_am_i(pos_ref, runs)
    rows[pl.ds(pl.multiple_of(core * SHARD, SHARD), SHARD), :] = own_ref[...]
    rows[pl.ds(pl.multiple_of((1 - core) * SHARD, SHARD), SHARD), :] = other_ref[...]
    return lead


def rope_for(half, cos_ref, sin_ref):
    lane = lax.broadcasted_iota(jnp.int32, (HALF, HEAD_DIM), 1)
    mine = (lane < HEAD_DIM // 2) if half == 0 else (lane >= HEAD_DIM // 2)
    cos, sin = cos_ref[...], sin_ref[...]
    cos = jnp.where(mine, cos, pltpu.roll(cos, HEAD_DIM // 2, 1))
    sin = jnp.where(mine, sin, pltpu.roll(sin, HEAD_DIM // 2, 1))
    sin = jnp.where(lane < HEAD_DIM // 2, -sin, sin)
    return lambda u: u * cos + pltpu.roll(u, HEAD_DIM // 2, 1) * sin


def key_kernel(half, runs, pos_ref, own_ref, other_ref, wk_ref, wv_ref, bk_ref, bv_ref, cos_ref, sin_ref,
               msg_ref, rows):
    lead = gather_rows(pos_ref, runs, own_ref, other_ref, rows)
    x = rows[...]
    rope = rope_for(half, cos_ref, sin_ref)
    keys = jnp.dot(x, wk_ref[...], preferred_element_type=F32) + bk_ref[...][None, :]
    msg_ref[0:HALF, :] = rope(keys).astype(BF16)
    values = jnp.dot(x, wv_ref[...], preferred_element_type=F32) + bv_ref[...][None, :]
    flipped = values.T.astype(BF16)
    msg_ref[HALF:HALF + SHARD, :] = flipped[:, 0:SHARD]
    msg_ref[HALF + SHARD:2 * HALF, :] = flipped[:, SHARD:HALF]
    msg_ref[2 * HALF:MSG, :] = jnp.full((TILE, HEAD_DIM), lead.astype(F32), F32).astype(BF16)


def query_kernel(half, runs, pos_ref, own_ref, other_ref, wq_ref, bq_ref, cos_ref, sin_ref, q_ref, rows):
    gather_rows(pos_ref, runs, own_ref, other_ref, rows)
    x = rows[...]
    rope = rope_for(half, cos_ref, sin_ref)
    for h in range(HEADS):
        cols = slice(h * HEAD_DIM, (h + 1) * HEAD_DIM)
        heads = jnp.dot(x, wq_ref[:, cols], preferred_element_type=F32) + bq_ref[cols][None, :]
        q_ref[:, h * HALF:(h + 1) * HALF] = rope(heads).T.astype(BF16)


def project_keys(half, runs, positions, own, other, weights, cos, sin):
    features = own.shape[1]
    return pl.pallas_call(
        functools.partial(key_kernel, half, runs),
        out_shape=jax.ShapeDtypeStruct((MSG, HEAD_DIM), BF16),
        in_specs=[SCALARS] + [WHOLE] * 8,
        out_specs=WHOLE,
        scratch_shapes=[pltpu.VMEM((HALF, features), BF16)],
        compiler_params=params(),
        cost_estimate=cost(4 * HALF * features * HEAD_DIM, 4 * features * HEAD_DIM),
    )(positions, own, other, *weights, cos, sin)


def project_queries(half, runs, positions, own, other, w_query, b_query, cos, sin):
    features = own.shape[1]
    return pl.pallas_call(
        functools.partial(query_kernel, half, runs),
        out_shape=jax.ShapeDtypeStruct((HEAD_DIM, HEADS * HALF), BF16),
        in_specs=[SCALARS] + [WHOLE] * 6,
        out_specs=WHOLE,
        scratch_shapes=[pltpu.VMEM((HALF, features), BF16)],
        compiler_params=params(),
        cost_estimate=cost(2 * HALF * features * HEADS * HEAD_DIM, 2 * features * HEADS * HEAD_DIM),
    )(positions, own, other, w_query, b_query, cos, sin)


def distance(kind, level, column):
    if kind == "up":
        return 4 * level + 0 * column
    if kind == "even":
        return 4 * level + column - lax.bitwise_xor(column, 1)
    if kind == "odd":
        return 4 * level + 2 * column - 3
    if kind == "cross":
        return 4 * level + jnp.where(column < 2, -2, 2)
    return jnp.where(column == 0, VISITS - 1, 0)


def visit(q_ref, msgs, state, at, first=False):
    k = msgs[at, 0:HALF, :]
    vt = jnp.concatenate([msgs[at, HALF:HALF + SHARD, :], msgs[at, HALF + SHARD:2 * HALF, :]], axis=1)
    for strip in range(HEADS * HALF // STRIP):
        cols = slice(strip * STRIP, (strip + 1) * STRIP)
        s = jnp.dot(k, q_ref[:, cols], preferred_element_type=F32)
        if first:
            key_at = lax.broadcasted_iota(jnp.int32, s.shape, 0)
            row_at = lax.broadcasted_iota(jnp.int32, s.shape, 1) + strip * STRIP % HALF
            s = jnp.where(key_at <= row_at, s, masked_score)
            peak = jnp.max(s, axis=0, keepdims=True)
        else:
            old = state[PEAK:PEAK + 1, cols]
            peak = jnp.maximum(old, jnp.max(s, axis=0, keepdims=True))
            factor = jnp.exp2((old - peak) * EXP_SCALE)
        expo = jnp.exp2((s - peak) * EXP_SCALE)
        total = jnp.sum(expo, axis=0, keepdims=True)
        mixed = jnp.dot(vt, expo.astype(BF16), preferred_element_type=F32)
        if not first:
            total = total + state[TOTAL:TOTAL + 1, cols] * factor
            mixed = mixed + state[0:HEAD_DIM, cols] * factor
        state[PEAK:PEAK + 1, cols] = peak
        state[TOTAL:TOTAL + 1, cols] = total
        state[0:HEAD_DIM, cols] = mixed


def attend_all(target, specs, places, arrays, pos_ref, runs, q_ref, msgs, state, todo, own=(), paired=False):
    lead, second, _ = where_am_i(pos_ref, runs)
    column = lax.bitwise_and(pos_ref[SHARD], 3)
    todo[0] = 0
    wanted = []
    for (half, kind, level), (which, index) in zip(specs, places):
        back = distance(kind, level, column)
        valid = jnp.logical_and(back >= 1, back <= VISITS - 1)
        role = second if half == 0 else 1 - second
        if half == target:
            run = jnp.max(arrays[which][index, 2 * HALF:MSG, :].astype(F32)).astype(jnp.int32)
            seen = jnp.where(role == 0, run < lead, run > lead)
        else:
            seen = role == 0
        wanted.append(jnp.logical_and(valid, seen))
    sources = [(arrays[which], index) for which, index in places]
    if own:
        msgs[0, :, :] = own[target][0, :, :]
        visit(q_ref, msgs, state, 0, True)
        wanted.append(second == 1 - target)
        sources.append((own[1 - target], 0))
    for want, (ref, index) in zip(wanted, sources):
        @pl.when(want)
        def _(ref=ref, index=index):
            place = todo[0]
            msgs[place, :, :] = ref[index, :, :]
            todo[0] = place + 1

    count = todo[0]

    def one(i, carry):
        visit(q_ref, msgs, state, i)
        return carry

    def two(i, carry):
        visit(q_ref, msgs, state, 2 * i)
        visit(q_ref, msgs, state, 2 * i + 1)
        return carry

    if paired:
        lax.fori_loop(0, lax.shift_right_logical(count, 1), two, 0)

        @pl.when(lax.bitwise_and(count, 1) == 1)
        def _():
            visit(q_ref, msgs, state, count - 1)
    else:
        lax.fori_loop(0, count, one, 0)


def attend_kernel(target, specs, places, own, paired, runs, pos_ref, q_ref, *rest):
    state, msgs, todo = rest[-3:]
    if own:
        attend_all(target, specs, places, rest[2:-3], pos_ref, runs, q_ref, msgs, state, todo, own=rest[:2])
    else:
        state[...] = rest[0][...]
        attend_all(target, specs, places, rest[1:-3], pos_ref, runs, q_ref, msgs, state, todo, paired=paired)


def unpack(messages):
    arrays, places, specs = [], [], []
    for half, kind, level, array, at in messages:
        for i, known in enumerate(arrays):
            if known is array:
                break
        else:
            i = len(arrays)
            arrays.append(array)
        places.append((i, at))
        specs.append((half, kind, level))
    return tuple(specs), tuple(places), arrays


def working(count):
    return [pltpu.VMEM((count, MSG, HEAD_DIM), BF16), pltpu.SMEM((1,), jnp.int32)]


def task_cost(count, more=0):
    return cost(count * 2 * HEADS * HALF * HALF * HEAD_DIM + more, 2**21, count * HEADS * HALF * HALF // 2)


def attend(target, messages, runs, positions, q, state=None, own=(), paired=False):
    specs, places, arrays = unpack(messages)
    before = list(own) if own else [state]
    return pl.pallas_call(
        functools.partial(attend_kernel, target, specs, places, bool(own), paired, runs),
        out_shape=jax.ShapeDtypeStruct((STATE, HEADS * HALF), F32),
        in_specs=[SCALARS] + [WHOLE] * (1 + len(before) + len(arrays)),
        out_specs=WHOLE,
        scratch_shapes=working(len(specs) + 1),
        compiler_params=params(),
        cost_estimate=task_cost(len(specs)),
    )(positions, q, *before, *arrays)


def project_out(pos_ref, runs, mixed, w_ref, keep_ref, send_ref):
    _, _, core = where_am_i(pos_ref, runs)
    keep_at = pl.ds(pl.multiple_of(core * SHARD, SHARD), SHARD)
    send_at = pl.ds(pl.multiple_of((1 - core) * SHARD, SHARD), SHARD)
    x = jnp.concatenate([mixed[send_at, :], mixed[keep_at, :]], axis=0)
    width = 512
    for j in range(w_ref.shape[1] // width):
        cols = slice(j * width, (j + 1) * width)
        part = jnp.dot(x, w_ref[:, cols], preferred_element_type=F32).astype(BF16)
        send_ref[:, cols] = part[0:SHARD]
        keep_ref[:, cols] = part[SHARD:HALF]


def last_kernel(target, specs, places, runs, pos_ref, q_ref, state_in, w_ref, *rest):
    keep_ref, send_ref, msgs, todo, state, mixed = rest[-6:]
    state[...] = state_in[...]
    attend_all(target, specs, places, rest[:-6], pos_ref, runs, q_ref, msgs, state, todo, paired=True)
    for h in range(HEADS):
        cols = slice(h * HALF, (h + 1) * HALF)
        scale = 1.0 / state[TOTAL:TOTAL + 1, cols]
        mixed[:, h * HEAD_DIM:(h + 1) * HEAD_DIM] = (state[0:HEAD_DIM, cols] * scale).T.astype(BF16)
    project_out(pos_ref, runs, mixed, w_ref, keep_ref, send_ref)


def attend_last(target, messages, runs, positions, q, state, w_out):
    specs, places, arrays = unpack(messages)
    part = jax.ShapeDtypeStruct((SHARD, w_out.shape[1]), BF16)
    return pl.pallas_call(
        functools.partial(last_kernel, target, specs, places, runs),
        out_shape=(part, part),
        in_specs=[SCALARS] + [WHOLE] * (3 + len(arrays)),
        out_specs=(WHOLE, WHOLE),
        scratch_shapes=working(len(specs)) + [pltpu.VMEM(state.shape, F32), pltpu.VMEM((HALF, HEADS * HEAD_DIM), BF16)],
        compiler_params=params(),
        cost_estimate=task_cost(len(specs), 2 * HALF * w_out.size),
    )(positions, q, state, w_out, *arrays)


def after(x, *earlier):
    return lax.optimization_barrier((x, *earlier))[0]


def local(tokens, norm_gain, w_query, b_query, w_key, b_key, w_value, b_value, w_out, positions):
    outer = lax.axis_size("outer")
    runs = 2 * outer

    def along(x, distance):
        return lax.ppermute(x, "outer", [(i, (i + distance) % outer) for i in range(outer)])

    def across(x, flip):
        return lax.ppermute(x, "inner", [(i, i ^ flip) for i in range(4)])

    far_tokens = across(tokens, 2)
    normed = normalize(tokens, norm_gain)
    near = across(normed, 1)

    run = positions[0] // HALF
    positions = jnp.concatenate([positions, lax.axis_index("outer")[None]])
    row = jnp.arange(HALF, dtype=jnp.int32)[:, None]
    lane = jnp.arange(HEAD_DIM, dtype=jnp.int32)[None, :]
    places = jnp.where(lane < HEAD_DIM // 2, run, runs - 1 - run) * HALF + row
    inverse = rope_base ** (-(jnp.arange(HEAD_DIM // 2, dtype=F32) * 2.0 / HEAD_DIM))
    angles = places.astype(F32) * jnp.concatenate([inverse, inverse])[None, :]
    cos, sin = jnp.cos(angles), jnp.sin(angles)

    kv = (w_key, w_value, b_key, b_value)
    ring = range(outer)

    def pack(*parts):
        return jnp.concatenate(parts, axis=0)

    def up(x):
        return along(x, 4)

    def even(x):
        return lax.ppermute(x, "outer", [(i, i ^ 1) for i in ring])

    def odd(x):
        return lax.ppermute(x, "outer", [(i, i ^ 3) for i in ring])

    def corner(x):
        return lax.ppermute(x, "outer", [(i, (i + 7 - 2 * (i % 4)) % outer) for i in ring if i % 4 >= 2])

    A, B = 0, 1

    a0 = project_keys(0, runs, positions, normed, near, kv, cos, sin)[None]
    a1, e0, o0 = up(a0), even(a0), odd(a0)
    qa = project_queries(0, runs, positions, after(normed, a0), near, w_query, b_query, cos, sin)

    far_tokens = after(far_tokens, qa, a1, e0, o0)
    far_near = normalize(across(far_tokens, 1), norm_gain)
    far = normalize(far_tokens, norm_gain)
    b0 = project_keys(1, runs, positions, far, far_near, kv, cos, sin)[None]
    u0 = pack(a1, b0)
    u1, e1, o1 = up(u0), even(pack(u0, o0)), odd(u0)
    qb = project_queries(1, runs, positions, after(far, b0), far_near, w_query, b_query, cos, sin)
    came1 = ((A, "up", 1, a1, 0), (A, "even", 0, e0, 0), (A, "odd", 0, o0, 0))
    state = attend(B, came1, runs, positions, qb, own=(a0, b0))

    v1 = after(u1, state)
    u2, e2, o2 = up(v1), even(pack(v1, o1[1:2])), odd(pack(v1, e1[0:1]))
    came2 = ((A, "up", 2, u1, 0), (B, "up", 1, u1, 1), (A, "even", 1, e1, 0), (B, "even", 0, e1, 1),
             (A, "cross", 0, e1, 2), (A, "odd", 1, o1, 0), (B, "odd", 0, o1, 1))
    state = attend(B, came2, runs, positions, qb, state)
    near_state = attend(A, came1, runs, positions, after(qa, state), own=(a0, b0))

    v2 = after(u2, near_state)
    u3, e3, o3 = up(pack(v2[1:2], o2[2:3])), even(pack(v2, o2[1:2])), odd(after(v2, e2, o2))
    came3 = ((A, "up", 3, u2, 0), (B, "up", 2, u2, 1), (A, "even", 2, e2, 0), (B, "even", 1, e2, 1),
             (B, "cross", 0, e2, 2), (A, "odd", 2, o2, 0), (B, "odd", 1, o2, 1), (A, "cross", 1, o2, 2))
    state = attend(B, came3, runs, positions, qb, state, paired=True)

    v3 = after(u3, state)
    u4, e4, o4 = up(pack(v3[1:2], o3[0:1])), even(pack(v3[0:1], o3[1:2])), odd(v3[0:1])
    c4 = corner(pack(v3[0:1], e3[1:2]))
    came4 = ((B, "up", 3, u3, 0), (A, "cross", 2, u3, 1), (A, "even", 3, e3, 0), (B, "even", 2, e3, 1),
             (B, "cross", 1, e3, 2), (A, "odd", 3, o3, 0), (B, "odd", 2, o3, 1))
    state = attend(B, came4, runs, positions, qb, state)
    near_state = attend(A, came2 + came3[:4], runs, positions, after(qa, state), near_state)
    came5 = ((B, "even", 3, e4, 0), (B, "cross", 2, e4, 1), (B, "odd", 3, o4, 0), (A, "cross", 3, u4, 0),
             (A, "corner", 3, u4, 1), (B, "corner", 3, c4, 0), (B, "cross", 3, c4, 1))

    keep_far, send_far = attend_last(B, came5, runs, positions, after(qb, near_state), state, w_out)
    got_far = across(send_far, 1)
    other = (keep_far.astype(F32) + got_far.astype(F32)).astype(BF16)
    arrived = across(other, 2)
    keep_near, send_near = attend_last(
        A, came3[4:] + came4 + came5, runs, positions, after(qa, other), near_state, w_out
    )
    got_near = across(send_near, 1)
    return (keep_near.astype(F32) + got_near.astype(F32) + arrived.astype(F32)).astype(BF16)


def solution(mesh):
    in_specs = (
        P(("outer", "inner"), None),
        P(),
        P(None, "inner"),
        P("inner"),
        P(None, "inner"),
        P("inner"),
        P(None, "inner"),
        P("inner"),
        P("inner", None),
        P(("outer", "inner")),
    )
    out_specs = P(("outer", "inner"), None)
    return jax.shard_map(local, mesh=mesh, in_specs=in_specs, out_specs=out_specs, check_vma=False)
```
